128 devices in a mesh: gx: 8 (over z, core), gy: 16 (over x, y).
Axes of the slice: x: 4, y: 4, z: 4, core: 2. Of those that a mesh axis runs over, the one named last changes fastest.
Arguments:
- residual: float32 [256, 8192], P('gy', 'gx'), may hold values from -60 to 60
- norm_gain: float32 [8192], P('gx'), may hold values from 0.1 to 1.9
- w_gate: bfloat16 [8192, 32768], P('gx', 'gy'), may hold values from -0.0625 to 0.0625
- w_up: bfloat16 [8192, 32768], P('gx', 'gy'), may hold values from -0.0625 to 0.0625
- w_query: bfloat16 [8192, 8192], P('gx', 'gy'), may hold values from -0.0625 to 0.0625
- w_keyval: bfloat16 [8192, 512], P('gx', 'gy'), may hold values from -0.19824219 to 0.19824219
- w_down: bfloat16 [32768, 8192], P('gy', 'gx'), may hold values from -0.03125 to 0.03125
- w_out: bfloat16 [8192, 8192], P('gy', 'gx'), may hold values from -0.0625 to 0.0625
- cache_keys: bfloat16 [256, 2048, 256], P(('gx', 'gy')), may hold values from -500 to 500
- cache_values: bfloat16 [256, 2048, 256], P(('gx', 'gy')), may hold values from -6 to 6
- lengths: int32 [256], P(('gx', 'gy')), may hold values from 1 to 2048, as said below
Outputs:
- final_stream: float32 [256, 8192], P('gy', 'gx')
The draws below stay inside these ranges and needn't reach their ends.
Inputs may be any that keep to these rules, and one draw needn't show every extreme that they name: `lengths`: row 0 uses all 2048 positions.
All inputs are finite; a program needn't handle non-finite values.
Results may differ from the reference program's by a relative error of at most 0.008.
Values may be sent and summed in bfloat16 or wider, within the bound.
No kernel may reach another device: no remote copies, remote signals or barrier semaphores. Data moves between devices by JAX's collectives and lax.ppermute only.
A program may use at most 64 MiB of HBM per device.

```python
import math
import jax
import jax.numpy as jnp
from jax import lax

D = 8192
FF = 32768
HEADS = 32
DH = 256
CACHE = 2048
STEPS = 2
ROWS = 256
QW = 8192


def column_spread(key, top):
    place = jnp.arange(D, dtype=jnp.float32) / float(max(D - 1, 1))
    rough = jax.random.uniform(key, (D,), jnp.float32, 0.7, 1.3)
    return jnp.exp(place * jnp.log(top)) * rough


def draw_residual(key, part):
    key = jax.random.fold_in(key, 23)
    spread = column_spread(jax.random.fold_in(key, 1), 6.0)
    base = jax.random.truncated_normal(jax.random.fold_in(key, 3), -4.0, 4.0, (ROWS, D), jnp.float32)
    return base * spread[None, :]


def draw_cache_keys(key, part):
    key = jax.random.fold_in(key, 11)
    base = jax.random.truncated_normal(key, -4.0, 4.0, (ROWS, CACHE, DH), jnp.float32) * 3.0
    return base.astype(jnp.bfloat16)


def draw_lengths(key, part):
    key = jax.random.fold_in(key, 5)
    drawn = jax.random.randint(key, (ROWS,), 1, CACHE + 1, dtype=jnp.int32)
    return drawn.at[0].set(CACHE)


def level_of(own_key, dims, split, least, high):
    factor_of, own = 1.0, jax.random.fold_in(own_key, 6)
    for axis_at, shards_of in split:
        heights = jnp.exp(jax.random.uniform(jax.random.fold_in(own, axis_at), (shards_of,), jnp.float32, least / len(split), high / len(split)))
        factor_of = factor_of * jnp.repeat(heights, dims[axis_at] // shards_of).reshape([-1 if axis == axis_at else 1 for axis in range(len(dims))])
    return factor_of


def normal_values(stream_key, extent, scale, limit, split=(), kind=jnp.bfloat16):
    loudness = level_of(stream_key, extent, split, -0.22, 0.18) if split else 1.0
    result = jax.random.normal(stream_key, extent, jnp.float32) * scale * loudness
    return jnp.minimum(jnp.maximum(result, -limit), limit).astype(kind)


def setup_inputs(seed: int = 0) -> dict:
    key_list = jax.random.split(jax.random.key(seed), 12)
    residual = draw_residual(jax.random.fold_in(key_list[11], 71), 0)
    norm_gain = jnp.clip(1.0 + 0.18 * jax.random.normal(key_list[1], (D,), jnp.float32), 0.1, 1.9)
    w_gate = normal_values(key_list[2], (D, FF), D ** -0.5, 0.0625, ((0, 8), (1, 16)))
    w_up = normal_values(key_list[3], (D, FF), D ** -0.5, 0.0625, ((0, 8), (1, 16)))
    w_query = normal_values(key_list[4], (D, QW), D ** -0.5, 0.0625, ((0, 8), (1, 16)))
    w_keyval = normal_values(key_list[5], (D, 2 * DH), (3.0 / D ** 0.5), 0.19824219, ((0, 8), (1, 16)))
    w_down = normal_values(key_list[6], (FF, D), FF ** -0.5, 0.03125, ((0, 16), (1, 8)))
    w_out = normal_values(key_list[7], (QW, D), QW ** -0.5, 0.0625, ((0, 16), (1, 8)))
    cache_keys = draw_cache_keys(jax.random.fold_in(key_list[11], 71), 0)
    cache_values = normal_values(key_list[9], (ROWS, CACHE, DH), 1.0, 6.0, ((0, 128),))
    lengths = draw_lengths(jax.random.fold_in(key_list[11], 71), 0)
    return dict(residual=residual, norm_gain=norm_gain, w_gate=w_gate, w_up=w_up, w_query=w_query, w_keyval=w_keyval, w_down=w_down, w_out=w_out, cache_keys=cache_keys, cache_values=cache_values, lengths=lengths)


EPS = 1e-06

def reference(residual, norm_gain, w_gate, w_up, w_query, w_keyval, w_down, w_out, cache_keys, cache_values, lengths):
    x = residual
    scale = 1.0 / math.sqrt(DH)
    positions = jnp.arange(CACHE, dtype=jnp.int32)
    live = positions[None, :] < lengths[:, None]
    keys_f = cache_keys.astype(jnp.float32)
    values_f = cache_values.astype(jnp.float32)
    fresh_keys = []
    fresh_values = []
    for step in range(STEPS):
        mean_sq = lax.optimization_barrier(jnp.mean(x * x, axis=1, keepdims=True))
        normed = (x * lax.rsqrt(mean_sq + EPS) * norm_gain[None, :]).astype(jnp.bfloat16)
        gate = jnp.dot(normed, w_gate, preferred_element_type=jnp.float32)
        up = jnp.dot(normed, w_up, preferred_element_type=jnp.float32)
        hidden = (jax.nn.silu(gate) * up).astype(jnp.bfloat16)
        query = jnp.dot(normed, w_query, preferred_element_type=jnp.float32).astype(jnp.bfloat16)
        keyval = jnp.dot(normed, w_keyval, preferred_element_type=jnp.float32).astype(jnp.bfloat16)
        fresh_keys.append(keyval[:, :DH])
        fresh_values.append(keyval[:, DH:])
        heads = query.reshape(ROWS, HEADS, DH).astype(jnp.float32)
        new_k = jnp.stack(fresh_keys, 1).astype(jnp.float32)
        new_v = jnp.stack(fresh_values, 1).astype(jnp.float32)
        old_s = jnp.einsum('rhd,rpd->rhp', heads, keys_f) * scale
        old_s = jnp.where(live[:, None, :], old_s, -jnp.inf)
        new_s = jnp.einsum('rhd,rtd->rht', heads, new_k) * scale
        top = jnp.maximum(lax.optimization_barrier(jnp.max(old_s, axis=2)), lax.optimization_barrier(jnp.max(new_s, axis=2)))
        old_e = jnp.exp(old_s - top[..., None])
        new_e = jnp.exp(new_s - top[..., None])
        total = lax.optimization_barrier(jnp.sum(old_e, axis=2)) + lax.optimization_barrier(jnp.sum(new_e, axis=2))
        old_w = (old_e / total[..., None]).astype(jnp.bfloat16)
        new_w = (new_e / total[..., None]).astype(jnp.bfloat16)
        old_w = lax.optimization_barrier(old_w).astype(jnp.float32)
        new_w = lax.optimization_barrier(new_w).astype(jnp.float32)
        attended = jnp.einsum('rhp,rpd->rhd', old_w, values_f) + jnp.einsum('rht,rtd->rhd', new_w, new_v)
        attended = attended.astype(jnp.bfloat16).reshape(ROWS, QW)
        x = x + jnp.dot(hidden, w_down, preferred_element_type=jnp.float32) + jnp.dot(attended, w_out, preferred_element_type=jnp.float32)
    return x
```

```python
import jax
import jax.numpy as jnp
from jax import lax
from jax.sharding import PartitionSpec as P

D = 8192
HEADS = 32
DH = 256
STEPS = 2
EPS = 1e-06
F32 = jnp.float32
BF16 = jnp.bfloat16


def dot32(a, b):
    return jnp.dot(a, b, preferred_element_type=F32)


def square_columns(squares, width):
    high = lax.reduce_precision(squares, 8, 7)
    low = squares - high
    pair = jnp.stack([high, low], axis=1)
    return jnp.pad(pair, ((0, 0), (0, width - 2))).astype(BF16)


def row_scale(columns):
    return lax.rsqrt((columns[..., 0:1] + columns[..., 1:2]) / D + EPS)


def attend(heads, key_list, value_list, cache_keys, cache_values, lengths):
    count = heads.shape[0]
    old_s = jnp.einsum("rhd,rpd->rhp", heads, cache_keys, preferred_element_type=F32)
    places = lax.broadcasted_iota(jnp.int32, (count, 1, cache_keys.shape[1]), 2)
    old_s = jnp.where(places < lengths[:, None, None], old_s, -jnp.inf)
    new_k = jnp.stack(key_list, 1)
    new_v = jnp.stack(value_list, 1)
    new_s = jnp.einsum("rhd,rtd->rht", heads, new_k, preferred_element_type=F32)
    top = jnp.maximum(jnp.max(old_s, axis=2), jnp.max(new_s, axis=2))
    old_e = jnp.exp(old_s - top[..., None])
    new_e = jnp.exp(new_s - top[..., None])
    total = jnp.sum(old_e, axis=2) + jnp.sum(new_e, axis=2)
    old_w = (old_e / total[..., None]).astype(BF16)
    new_w = (new_e / total[..., None]).astype(BF16)
    result = jnp.einsum("rhp,rpd->rhd", old_w, cache_values, preferred_element_type=F32)
    result = result + jnp.einsum("rht,rtd->rhd", new_w, new_v, preferred_element_type=F32)
    return result.astype(BF16)


def make_body(gx, gy):
    gz = gx // 2
    core_swap = [(n, n ^ 1) for n in range(gx)]
    z_groups = [[2 * z + c for z in range(gz)] for c in range(2)]

    def exchange(parts, axis, groups=None):
        return lax.all_to_all(
            parts, axis, split_axis=0, concat_axis=0, tiled=False, axis_index_groups=groups
        )

    def body(
        residual,
        norm_gain,
        w_gate,
        w_up,
        w_query,
        w_keyval,
        w_down,
        w_out,
        cache_keys,
        cache_values,
        lengths,
    ):
        stream = residual
        own_rows, width = residual.shape
        rows = own_rows * gy
        ff_cols = w_gate.shape[1]
        half = ff_cols // 2
        q_cols = w_query.shape[1]
        kv_cols = w_keyval.shape[1]
        cache_rows = cache_keys.shape[0]
        first = lax.axis_index("gx") % 2 == 0
        inverse_gain = 1.0 / norm_gain
        key_list = []
        value_list = []
        for step in range(STEPS):
            scaled = (stream * norm_gain[None, :]).astype(BF16)
            gathered = exchange(jnp.broadcast_to(scaled[None], (gy, own_rows, width)), "gy")
            gathered = gathered.reshape(rows, width)

            plain = gathered.astype(F32) * inverse_gain[None, :]
            squares = square_columns(jnp.sum(plain * plain, axis=1), 128)
            query_part = dot32(gathered, w_query).astype(BF16)
            keyval_part = dot32(gathered, w_keyval).astype(BF16)
            packed = jnp.concatenate(
                [query_part, keyval_part, squares[:, : 128 - kv_cols]], axis=1
            )
            packed = exchange(packed.reshape(gx * gy, cache_rows, q_cols + 128), ("gx", "gy"))

            gate_part = dot32(gathered, w_gate).astype(BF16)
            up_part = dot32(gathered, w_up).astype(BF16)
            keep = jnp.concatenate(
                [
                    jnp.where(first, gate_part[:, :half], gate_part[:, half:]),
                    jnp.where(first, up_part[:, :half], up_part[:, half:]),
                    squares,
                ],
                axis=1,
            )
            give = jnp.concatenate(
                [
                    jnp.where(first, gate_part[:, half:], gate_part[:, :half]),
                    jnp.where(first, up_part[:, half:], up_part[:, :half]),
                    squares,
                ],
                axis=1,
            )
            other = lax.ppermute(give, "gx", core_swap)
            pair = (keep.astype(F32) + other.astype(F32)).astype(BF16)
            pair = exchange(pair.reshape(gz, rows // gz, 2 * half + 128), "gx", z_groups)

            mine = jnp.sum(
                packed.reshape(gx, gy, cache_rows, q_cols + 128).astype(F32), axis=0
            )
            mine = mine * row_scale(mine[0, :, q_cols + kv_cols :])[None]
            query = mine[:, :, :q_cols].astype(BF16).transpose(1, 0, 2)
            query = query.reshape(cache_rows, HEADS, DH) * BF16(DH**-0.5)
            keyval = mine[:, :, q_cols : q_cols + kv_cols].astype(BF16).transpose(1, 0, 2)
            keyval = keyval.reshape(cache_rows, 2 * DH)
            key_list.append(keyval[:, :DH])
            value_list.append(keyval[:, DH:])
            attended = attend(query, key_list, value_list, cache_keys, cache_values, lengths)
            blocks = attended.reshape(cache_rows, gy, q_cols).transpose(1, 0, 2)
            blocks = jnp.broadcast_to(blocks[None], (gx, gy, cache_rows, q_cols))
            heads_all = exchange(blocks.reshape(gx * gy, cache_rows, q_cols), ("gx", "gy"))
            heads_all = heads_all.reshape(rows, q_cols)

            summed = jnp.sum(pair.astype(F32), axis=0)
            scale = row_scale(summed[:, 2 * half :])
            gate = summed[:, :half] * scale
            up = summed[:, half : 2 * half] * scale
            hidden = (jax.nn.silu(gate) * up).astype(BF16)
            hidden = exchange(
                jnp.broadcast_to(hidden[None], (gz,) + hidden.shape), "gx", z_groups
            ).reshape(rows, half)
            hidden_other = lax.ppermute(hidden, "gx", core_swap)
            hidden_all = jnp.concatenate(
                [
                    jnp.where(first, hidden, hidden_other),
                    jnp.where(first, hidden_other, hidden),
                ],
                axis=1,
            )
            delta = (dot32(hidden_all, w_down) + dot32(heads_all, w_out)).astype(BF16)
            delta = exchange(delta.reshape(gy, own_rows, width), "gy")
            stream = stream + jnp.sum(delta.astype(F32), axis=0)
        return stream

    return body


def solution(mesh):
    in_specs = (
        P("gy", "gx"),
        P("gx"),
        P("gx", "gy"),
        P("gx", "gy"),
        P("gx", "gy"),
        P("gx", "gy"),
        P("gy", "gx"),
        P("gy", "gx"),
        P(("gx", "gy"), None, None),
        P(("gx", "gy"), None, None),
        P(("gx", "gy")),
    )
    return jax.shard_map(
        make_body(mesh.shape["gx"], mesh.shape["gy"]),
        mesh=mesh,
        in_specs=in_specs,
        out_specs=P("gy", "gx"),
        check_vma=False,
    )
```

```python
import functools

import jax
import jax.numpy as jnp
from jax import lax
from jax.experimental import pallas as pl
from jax.experimental.pallas import tpu as pltpu
from jax.sharding import PartitionSpec as P

D = 8192
HEADS = 32
DH = 256
STEPS = 2
EPS = 1e-06
LANES = 128
F32 = jnp.float32
BF16 = jnp.bfloat16
PARAMS = pltpu.CompilerParams(vmem_limit_bytes=16 * 1024 * 1024)
VMEM = pl.BlockSpec(memory_space=pltpu.VMEM)
SMEM = pl.BlockSpec(memory_space=pltpu.SMEM)
COST = pl.CostEstimate(flops=0, bytes_accessed=0, transcendentals=0)
LATE = pl.CostEstimate(flops=10**10, bytes_accessed=0, transcendentals=0)


def dot32(a, b):
    return jnp.dot(a, b, preferred_element_type=F32)


def call(kernel, out_shape, *args, scalars=0, cost=COST, **kwargs):
    return pl.pallas_call(
        kernel,
        out_shape=out_shape,
        in_specs=[SMEM] * scalars + [VMEM] * (len(args) - scalars),
        compiler_params=PARAMS,
        cost_estimate=cost,
        **kwargs,
    )(*args)


def stream_call(kernel, out_shape, scalars, grid, specs, args, out_specs, cost=COST, scratch=()):
    return pl.pallas_call(
        kernel,
        out_shape=out_shape,
        grid_spec=pltpu.PrefetchScalarGridSpec(
            num_scalar_prefetch=len(scalars),
            grid=grid,
            in_specs=specs,
            out_specs=out_specs,
            scratch_shapes=scratch,
        ),
        compiler_params=PARAMS,
        cost_estimate=cost,
    )(*scalars, *args)


def whole(array):
    return pl.BlockSpec(array.shape, lambda *_: (0,) * array.ndim)


def spread_kernel(x_ref, gain_ref, out_ref):
    scaled = (x_ref[...] * gain_ref[...]).astype(BF16)
    for n in range(out_ref.shape[0]):
        out_ref[n] = scaled


def add_kernel(x_ref, delta_ref, gain_ref, new_ref, out_ref=None):
    new = x_ref[...] + jnp.sum(delta_ref[...].astype(F32), axis=0)
    new_ref[...] = new
    if out_ref is not None:
        scaled = (new * gain_ref[...]).astype(BF16)
        for n in range(out_ref.shape[0]):
            out_ref[n] = scaled


def query_kernel(kv_cols, x_ref, inverse_ref, wq_ref, wkv_ref, out_ref, squares_ref):
    x = x_ref[...]
    plain = x.astype(F32) * inverse_ref[...]
    squares = jnp.sum(plain * plain, axis=1, keepdims=True)
    high = squares.astype(BF16).astype(F32)
    low = squares - high
    lane = lax.broadcasted_iota(jnp.int32, squares_ref.shape, 1)
    columns = jnp.where(lane == kv_cols, high, jnp.where(lane == kv_cols + 1, low, 0.0))
    squares_ref[...] = columns.astype(BF16)
    q_cols = wq_ref.shape[1]
    out_ref[:, :q_cols] = dot32(x, wq_ref[...]).astype(BF16)
    out_ref[:, q_cols:] = (dot32(x, wkv_ref[...]) + columns).astype(BF16)


def hidden_part_kernel(half_ref, x_ref, wg_ref, wu_ref, *outs):
    for n in range(len(outs) // 2):

        @pl.when(pl.program_id(0) == n)
        def _():
            outs[2 * n][...] = dot32(x_ref[...], wg_ref[...]).astype(BF16)
            outs[2 * n + 1][...] = dot32(x_ref[...], wu_ref[...]).astype(BF16)


def hidden_part(half_index, x, w_gate, w_up, blocks=2):
    rows, width = x.shape
    block = w_gate.shape[1] // 2 // blocks
    weight = pl.BlockSpec((width, block), lambda n, h: (0, h[0] * blocks + n))
    part = jax.ShapeDtypeStruct((rows, block), BF16)
    return stream_call(
        hidden_part_kernel,
        [part] * (2 * blocks),
        [half_index],
        (blocks,),
        [whole(x), weight, weight],
        [x, w_gate, w_up],
        [whole(part)] * (2 * blocks),
    )


def pair_kernel(gz, z_ref, *refs):
    outs = refs[-gz:]
    count = (len(refs) - gz) // 2
    half = sum(ref.shape[1] for ref in refs[: count - 1]) // 2
    size = outs[0].shape[0]
    for n in range(gz):
        here = pl.ds(pl.multiple_of(lax.rem(z_ref[0] + n, gz) * size, size), size)
        for k in range(count):
            keep, other = refs[k], refs[count + k]
            block = keep.shape[1]
            at = 2 * half if k == count - 1 else k % 2 * half + k // 2 * block
            outs[n][:, at : at + block] = (
                keep[here, :].astype(F32) + other[here, :].astype(F32)
            ).astype(BF16)


def hidden_kernel(kv_cols, *refs):
    out_ref = refs[-1]
    half = out_ref.shape[1]
    total = refs[0][...].astype(F32)
    for ref in refs[1:-1]:
        total = total + ref[...].astype(F32)
    at = 2 * half + kv_cols
    scale = lax.rsqrt((total[:, at : at + 1] + total[:, at + 1 : at + 2]) / D + EPS)
    gate = total[:, :half] * scale
    up = total[:, half : 2 * half] * scale
    out_ref[...] = (gate / (1.0 + jnp.exp(-gate)) * up).astype(BF16)


def attend_kernel(steps, lengths_ref, q_ref, *refs):
    news = refs[:steps]
    keys_ref, values_ref, out_ref = refs[steps:]
    row = pl.program_id(0)
    scale = DH**-0.5
    q = q_ref[0]
    heads = jnp.concatenate([q[:, :DH], q[:, DH:]], axis=0)
    old_s = lax.dot_general(
        heads, keys_ref[0], (((1,), (1,)), ((), ())), preferred_element_type=F32
    )
    place = lax.broadcasted_iota(jnp.int32, old_s.shape, 1)
    old_s = jnp.where(place < lengths_ref[row], old_s * scale, -jnp.inf)
    heads32 = heads.astype(F32)
    top = jnp.max(old_s, axis=1, keepdims=True)
    new_s = []
    new_v = []
    for ref in news:
        line = ref[pl.ds(row, 1), :]
        score = jnp.sum(heads32 * line[:, :DH], axis=1, keepdims=True) * scale
        new_s.append(score)
        new_v.append(line[:, DH:])
        top = jnp.maximum(top, score)
    old_e = jnp.exp(old_s - top)
    new_e = [jnp.exp(score - top) for score in new_s]
    total = jnp.sum(old_e, axis=1, keepdims=True)
    for e in new_e:
        total = total + e
    old_w = (old_e / total).astype(BF16)
    result = dot32(old_w, values_ref[0])
    for e, v in zip(new_e, new_v):
        result = result + (e / total).astype(BF16).astype(F32) * v
    count = q.shape[0]
    out_ref[0] = jnp.concatenate([result[:count], result[count:]], axis=1).astype(BF16)


def attend(lengths, query, news, keys, values):
    def by_row(array):
        return pl.BlockSpec((1,) + array.shape[1:], lambda r, n: (r, 0, 0))

    return stream_call(
        functools.partial(attend_kernel, len(news)),
        jax.ShapeDtypeStruct(query.shape, BF16),
        [lengths],
        (query.shape[0],),
        [by_row(query)] + [whole(new) for new in news] + [by_row(keys), by_row(values)],
        [query, *news, keys, values],
        by_row(query),
    )


def heads_kernel(heads_ref, wout_ref, out_ref):
    out_ref[...] = dot32(heads_ref[...], wout_ref[...])


def heads_output(heads, w_out, blocks=2):
    rows, q_cols = heads.shape
    width = w_out.shape[1]
    return stream_call(
        heads_kernel,
        jax.ShapeDtypeStruct((rows, width), F32),
        [],
        (blocks,),
        [whole(heads), pl.BlockSpec((q_cols, width // blocks), lambda n: (0, n))],
        [heads, w_out],
        pl.BlockSpec((rows, width // blocks), lambda n: (0, n)),
        cost=LATE,
    )


def output_kernel(gz, place_ref, *refs):
    pieces, others = refs[:gz], refs[gz : 2 * gz]
    heads_ref, down_ref, out_ref, hidden = refs[2 * gz :]
    size, half = pieces[0].shape

    @pl.when(pl.program_id(0) == 0)
    def _():
        z, c = place_ref[0], place_ref[1]
        mine = pl.ds(pl.multiple_of(c * half, half), half)
        theirs = pl.ds(pl.multiple_of((1 - c) * half, half), half)
        for n in range(gz):
            at = pl.ds(pl.multiple_of(lax.rem(z + gz - n, gz) * size, size), size)
            hidden[at, mine] = pieces[n][...]
            hidden[at, theirs] = others[n][...]

    out_ref[...] = (dot32(hidden[...], down_ref[...]) + heads_ref[...]).astype(BF16)


def output_part(place, pieces, others, heads_part, w_down, blocks=4):
    rows, width = heads_part.shape
    ff_cols = w_down.shape[0]
    block = width // blocks
    return stream_call(
        functools.partial(output_kernel, len(pieces)),
        jax.ShapeDtypeStruct((rows, width), BF16),
        [place],
        (blocks,),
        [whole(piece) for piece in pieces + others]
        + [
            pl.BlockSpec((rows, block), lambda n, p: (0, n)),
            pl.BlockSpec((ff_cols, block), lambda n, p: (0, n)),
        ],
        [*pieces, *others, heads_part, w_down],
        pl.BlockSpec((rows, block), lambda n, p: (0, n)),
        scratch=[pltpu.VMEM((rows, ff_cols), BF16)],
    )


def make_body(gx, gy):
    gz = gx // 2
    core_swap = [(n, n ^ 1) for n in range(gx)]

    def z_shift(n):
        return [(2 * z + c, 2 * ((z + n) % gz) + c) for z in range(gz) for c in range(2)]

    def exchange(parts, axis):
        return lax.all_to_all(parts, axis, split_axis=0, concat_axis=0, tiled=False)

    def body(
        residual,
        norm_gain,
        w_gate,
        w_up,
        w_query,
        w_keyval,
        w_down,
        w_out,
        cache_keys,
        cache_values,
        lengths,
    ):
        stream = residual
        own_rows, width = residual.shape
        rows = own_rows * gy
        half = w_gate.shape[1] // 2
        q_cols = w_query.shape[1]
        kv_cols = w_keyval.shape[1]
        cache_rows = cache_keys.shape[0]
        me = lax.axis_index("gx")
        z, core = me // 2, lax.rem(me, 2)
        place = jnp.stack([z, core]).astype(jnp.int32)
        gain = norm_gain[None, :]
        inverse_gain = 1.0 / gain
        keyval_padded = jnp.pad(w_keyval, ((0, 0), (0, LANES - kv_cols)))
        news = []
        spread = call(
            spread_kernel, jax.ShapeDtypeStruct((gy, own_rows, width), BF16), stream, gain
        )
        w_gate, w_up, w_query, w_down, w_out, cache_keys, cache_values = [
            pltpu.with_memory_space_constraint(array, pltpu.HBM)
            for array in (w_gate, w_up, w_query, w_down, w_out, cache_keys, cache_values)
        ]
        for step in range(STEPS):
            gathered = exchange(spread, "gy").reshape(rows, width)
            packed, squares = call(
                functools.partial(query_kernel, kv_cols),
                (
                    jax.ShapeDtypeStruct((rows, q_cols + LANES), BF16),
                    jax.ShapeDtypeStruct((rows, LANES), BF16),
                ),
                gathered,
                inverse_gain,
                w_query,
                keyval_padded,
            )
            packed = exchange(
                packed.reshape(gx * gy, cache_rows, q_cols + LANES), ("gx", "gy")
            )

            give = hidden_part(place[1:] ^ 1, gathered, w_gate, w_up)
            other = [lax.ppermute(part, "gx", core_swap) for part in (*give, squares)]
            keep = hidden_part(place[1:], gathered, w_gate, w_up)
            pair = call(
                functools.partial(pair_kernel, gz),
                [jax.ShapeDtypeStruct((rows // gz, 2 * half + LANES), BF16)] * gz,
                place,
                *keep,
                squares,
                *other,
                scalars=1,
            )
            arrived = [pair[0]] + [lax.ppermute(pair[n], "gx", z_shift(n)) for n in range(1, gz)]

            packed = lax.optimization_barrier((packed, pair[0]))[0]
            mine = jnp.sum(
                packed.reshape(gx, gy, cache_rows, q_cols + LANES).astype(F32), axis=0
            ).transpose(1, 0, 2)
            at = q_cols + kv_cols
            scale = lax.rsqrt((mine[:, :1, at : at + 1] + mine[:, :1, at + 1 : at + 2]) / D + EPS)
            query = (mine[:, :, :q_cols] * scale).astype(BF16)
            keyval = (mine[:, :, q_cols:at] * scale).astype(BF16).astype(F32)
            news.append(keyval.reshape(cache_rows, 2 * DH))
            attended = attend(lengths, query, news, cache_keys, cache_values)
            blocks = attended.transpose(1, 0, 2)
            blocks = jnp.broadcast_to(blocks[None], (gx, gy, cache_rows, q_cols))
            blocks = blocks.reshape(gx * gy, cache_rows, q_cols)
            heads_all = exchange(blocks, ("gx", "gy")).reshape(rows, q_cols)
            heads_part = heads_output(heads_all, w_out)

            arrived = lax.optimization_barrier((arrived, blocks))[0]
            hidden = call(
                functools.partial(hidden_kernel, kv_cols),
                jax.ShapeDtypeStruct((rows // gz, half), BF16),
                *arrived,
            )
            pieces = [hidden] + [lax.ppermute(hidden, "gx", z_shift(n)) for n in range(1, gz)]
            others = [lax.ppermute(piece, "gx", core_swap) for piece in pieces]
            delta = output_part(place, pieces, others, heads_part, w_down)
            delta = exchange(delta.reshape(gy, own_rows, width), "gy")
            stream_shape = jax.ShapeDtypeStruct(stream.shape, F32)
            spread_shape = jax.ShapeDtypeStruct((gy, own_rows, width), BF16)
            if step + 1 < STEPS:
                stream, spread = call(
                    add_kernel, (stream_shape, spread_shape), stream, delta, gain
                )
            else:
                stream = call(add_kernel, stream_shape, stream, delta, gain)
        return stream

    return body


def solution(mesh):
    in_specs = (
        P("gy", "gx"),
        P("gx"),
        P("gx", "gy"),
        P("gx", "gy"),
        P("gx", "gy"),
        P("gx", "gy"),
        P("gy", "gx"),
        P("gy", "gx"),
        P(("gx", "gy"), None, None),
        P(("gx", "gy"), None, None),
        P(("gx", "gy")),
    )
    return jax.shard_map(
        make_body(mesh.shape["gx"], mesh.shape["gy"]),
        mesh=mesh,
        in_specs=in_specs,
        out_specs=P("gy", "gx"),
        check_vma=False,
    )
```

```python
import functools

import jax
import jax.numpy as jnp
from jax import lax
from jax.experimental import pallas as pl
from jax.experimental.pallas import tpu as pltpu
from jax.sharding import PartitionSpec as P

D = 8192
HEADS = 32
DH = 256
STEPS = 2
EPS = 1e-06
LANES = 128
F32 = jnp.float32
BF16 = jnp.bfloat16
PARAMS = pltpu.CompilerParams(vmem_limit_bytes=16 * 1024 * 1024)
VMEM = pl.BlockSpec(memory_space=pltpu.VMEM)
SMEM = pl.BlockSpec(memory_space=pltpu.SMEM)
COST = pl.CostEstimate(flops=0, bytes_accessed=0, transcendentals=0)
LATE = pl.CostEstimate(flops=10**10, bytes_accessed=0, transcendentals=0)


def dot32(a, b):
    return jnp.dot(a, b, preferred_element_type=F32)


HBM = pl.BlockSpec(memory_space=pltpu.HBM)


def call(kernel, out_shape, *args, scalars=0, far=0, copies=0, buffers=(), cost=COST):
    near = len(args) - scalars - far
    far_args = [pltpu.with_memory_space_constraint(a, pltpu.HBM) for a in args[scalars + near :]]
    scratch = list(buffers)
    if copies:
        scratch.append(pltpu.SemaphoreType.DMA((copies,)))
    return pl.pallas_call(
        kernel,
        out_shape=out_shape,
        in_specs=[SMEM] * scalars + [VMEM] * near + [HBM] * far,
        scratch_shapes=scratch,
        compiler_params=PARAMS,
        cost_estimate=cost,
    )(*args[: scalars + near], *far_args)


def start_copies(pairs, sems):
    copies = [
        pltpu.make_async_copy(source, target, sems.at[n]) for n, (source, target) in enumerate(pairs)
    ]
    for copy in copies:
        copy.start()
    return copies


def spread_kernel(x_ref, gain_ref, out_ref, x, gain, sems):
    for copy in start_copies([(x_ref, x), (gain_ref, gain)], sems):
        copy.wait()
    scaled = (x[...] * gain[...]).astype(BF16)
    for n in range(out_ref.shape[0]):
        out_ref[n] = scaled


def add_kernel(x_ref, delta_ref, gain_ref, new_ref, out_ref=None):
    new = x_ref[...] + jnp.sum(delta_ref[...].astype(F32), axis=0)
    new_ref[...] = new
    if out_ref is not None:
        scaled = (new * gain_ref[...]).astype(BF16)
        for n in range(out_ref.shape[0]):
            out_ref[n] = scaled


def query_kernel(kv_cols, x_ref, inverse_ref, wkv_ref, wq_ref, out_ref, squares_ref):
    x = x_ref[...]
    plain = x.astype(F32) * inverse_ref[...]
    squares = jnp.sum(plain * plain, axis=1, keepdims=True)
    high = squares.astype(BF16).astype(F32)
    low = squares - high
    lane = lax.broadcasted_iota(jnp.int32, squares_ref.shape, 1)
    columns = jnp.where(lane == kv_cols, high, jnp.where(lane == kv_cols + 1, low, 0.0))
    squares_ref[...] = columns.astype(BF16)
    q_cols = wq_ref.shape[1]
    out_ref[:, :q_cols] = dot32(x, wq_ref[...]).astype(BF16)
    out_ref[:, q_cols:] = (dot32(x, wkv_ref[...]) + columns).astype(BF16)


def hidden_part_kernel(half_ref, x_ref, wg_ref, wu_ref, *outs):
    block = wg_ref.shape[1]
    wide = outs[0].shape[1]
    for n in range(len(outs) // 2 * (wide // block)):

        @pl.when(pl.program_id(0) == n)
        def _():
            at = n * block
            for k, ref in enumerate((wg_ref, wu_ref)):
                outs[at // wide * 2 + k][:, at % wide : at % wide + block] = dot32(
                    x_ref[...], ref[...]
                ).astype(BF16)


def hidden_part(half_index, x, w_gate, w_up, outs=2, blocks=2):
    rows, width = x.shape
    half = w_gate.shape[1] // 2
    weight = pl.BlockSpec((width, half // blocks), lambda n, h: (0, h[0] * blocks + n))
    part = jax.ShapeDtypeStruct((rows, half // outs), BF16)
    return pl.pallas_call(
        hidden_part_kernel,
        out_shape=[part] * (2 * outs),
        grid_spec=pltpu.PrefetchScalarGridSpec(
            num_scalar_prefetch=1,
            grid=(blocks,),
            in_specs=[pl.BlockSpec(x.shape, lambda n, h: (0, 0)), weight, weight],
            out_specs=[pl.BlockSpec(part.shape, lambda n, h: (0, 0))] * (2 * outs),
        ),
        compiler_params=PARAMS,
        cost_estimate=COST,
    )(
        half_index,
        x,
        pltpu.with_memory_space_constraint(w_gate, pltpu.HBM),
        pltpu.with_memory_space_constraint(w_up, pltpu.HBM),
    )


def pair_kernel(gz, z_ref, *refs):
    outs = refs[-gz:]
    count = (len(refs) - gz) // 2
    half = sum(ref.shape[1] for ref in refs[: count - 1]) // 2
    size = outs[0].shape[0]
    for n in range(gz):
        here = pl.ds(pl.multiple_of(lax.rem(z_ref[0] + n, gz) * size, size), size)
        for k in range(count):
            keep, other = refs[k], refs[count + k]
            block = keep.shape[1]
            at = 2 * half if k == count - 1 else k % 2 * half + k // 2 * block
            outs[n][:, at : at + block] = (
                keep[here, :].astype(F32) + other[here, :].astype(F32)
            ).astype(BF16)


def hidden_kernel(kv_cols, *refs):
    out_ref = refs[-1]
    half = out_ref.shape[1]
    total = refs[0][...].astype(F32)
    for ref in refs[1:-1]:
        total = total + ref[...].astype(F32)
    at = 2 * half + kv_cols
    scale = lax.rsqrt((total[:, at : at + 1] + total[:, at + 1 : at + 2]) / D + EPS)
    gate = total[:, :half] * scale
    up = total[:, half : 2 * half] * scale
    out_ref[...] = (gate / (1.0 + jnp.exp(-gate)) * up).astype(BF16)


def attend_kernel(steps, lengths_ref, q_ref, *refs):
    news = refs[:steps]
    keys_ref, values_ref, out_ref, keys, values, sems = refs[steps:]
    rows = q_ref.shape[0]
    key_copies = start_copies(
        [(keys_ref.at[row], keys.at[row]) for row in range(rows)], sems.at[:rows]
    )
    scale = DH**-0.5
    heads, scores, new_scores, new_values = [], [], [], []
    for row in range(rows):
        q = q_ref[row]
        heads.append(jnp.concatenate([q[:, :DH], q[:, DH:]], axis=0))
        heads32 = heads[row].astype(F32)
        lines = [ref[row : row + 1, :] for ref in news]
        new_scores.append(
            [jnp.sum(heads32 * line[:, :DH], axis=1, keepdims=True) * scale for line in lines]
        )
        new_values.append([line[:, DH:] for line in lines])
    for copy in key_copies:
        copy.wait()
    value_copies = start_copies(
        [(values_ref.at[row], values.at[row]) for row in range(rows)], sems.at[rows:]
    )
    for row in range(rows):
        old_s = lax.dot_general(
            heads[row], keys[row], (((1,), (1,)), ((), ())), preferred_element_type=F32
        )
        place = lax.broadcasted_iota(jnp.int32, old_s.shape, 1)
        scores.append(jnp.where(place < lengths_ref[row], old_s * scale, -jnp.inf))
    weights = []
    for row in range(rows):
        top = jnp.max(scores[row], axis=1, keepdims=True)
        for score in new_scores[row]:
            top = jnp.maximum(top, score)
        old_e = jnp.exp(scores[row] - top)
        new_e = [jnp.exp(score - top) for score in new_scores[row]]
        total = jnp.sum(old_e, axis=1, keepdims=True)
        for e in new_e:
            total = total + e
        weights.append(((old_e / total).astype(BF16), [(e / total).astype(BF16) for e in new_e]))
    for copy in value_copies:
        copy.wait()
    for row in range(rows):
        old_w, new_w = weights[row]
        result = dot32(old_w, values[row])
        for w, v in zip(new_w, new_values[row]):
            result = result + w.astype(F32) * v
        count = q_ref.shape[1]
        out_ref[row] = jnp.concatenate([result[:count], result[count:]], axis=1).astype(BF16)


def attend(lengths, query, news, keys, values):
    return call(
        functools.partial(attend_kernel, len(news)),
        jax.ShapeDtypeStruct(query.shape, BF16),
        lengths,
        query,
        *news,
        keys,
        values,
        scalars=1,
        far=2,
        copies=2 * keys.shape[0],
        buffers=[pltpu.VMEM(keys.shape, BF16), pltpu.VMEM(values.shape, BF16)],
    )


def heads_kernel(blocks, heads_ref, wout_ref, down_ref, out_ref, held_ref, buffer, sems):
    width = out_ref.shape[1]
    block = width // blocks
    spots = [pl.ds(at, block) for at in range(0, width, block)]
    pairs = [(wout_ref.at[:, spot], buffer.at[:, spot]) for spot in spots]
    pairs += [(down_ref.at[:, spot], held_ref.at[:, spot]) for spot in spots]
    copies = start_copies(pairs, sems)
    for n, spot in enumerate(spots):
        copies[n].wait()
        out_ref[:, spot] = dot32(heads_ref[...], buffer[:, spot])
    for copy in copies[blocks:]:
        copy.wait()


def heads_output(heads, w_out, w_down, blocks=4):
    width = w_out.shape[1]
    return call(
        functools.partial(heads_kernel, blocks),
        [
            jax.ShapeDtypeStruct((heads.shape[0], width), F32),
            pltpu.VMEM(w_down.shape, w_down.dtype),
        ],
        heads,
        w_out,
        w_down,
        far=2,
        copies=2 * blocks,
        buffers=[pltpu.VMEM(w_out.shape, BF16)],
        cost=LATE,
    )


def output_kernel(gz, block, place_ref, *refs):
    pieces, others = refs[:gz], refs[gz : 2 * gz]
    heads_ref, down_ref, out_ref, hidden = refs[2 * gz :]
    size, half = pieces[0].shape
    z, c = place_ref[0], place_ref[1]
    mine = pl.ds(pl.multiple_of(c * half, half), half)
    theirs = pl.ds(pl.multiple_of((1 - c) * half, half), half)
    for n in range(gz):
        at = pl.ds(pl.multiple_of(lax.rem(z + gz - n, gz) * size, size), size)
        hidden[at, mine] = pieces[n][...]
        hidden[at, theirs] = others[n][...]
    for at in range(0, out_ref.shape[1], block):
        out_ref[:, at : at + block] = (
            dot32(hidden[...], down_ref[:, at : at + block]) + heads_ref[:, at : at + block]
        ).astype(BF16)


def output_part(place, pieces, others, heads_part, w_down):
    return call(
        functools.partial(output_kernel, len(pieces), 512),
        jax.ShapeDtypeStruct(heads_part.shape, BF16),
        place,
        *pieces,
        *others,
        heads_part,
        w_down,
        scalars=1,
        buffers=[pltpu.VMEM((heads_part.shape[0], w_down.shape[0]), BF16)],
    )


def make_body(gx, gy):
    gz = gx // 2
    core_swap = [(n, n ^ 1) for n in range(gx)]

    def z_shift(n):
        return [(2 * z + c, 2 * ((z + n) % gz) + c) for z in range(gz) for c in range(2)]

    def exchange(parts, axis):
        return lax.all_to_all(parts, axis, split_axis=0, concat_axis=0, tiled=False)

    def body(
        residual,
        norm_gain,
        w_gate,
        w_up,
        w_query,
        w_keyval,
        w_down,
        w_out,
        cache_keys,
        cache_values,
        lengths,
    ):
        stream = residual
        own_rows, width = residual.shape
        rows = own_rows * gy
        half = w_gate.shape[1] // 2
        q_cols = w_query.shape[1]
        kv_cols = w_keyval.shape[1]
        cache_rows = cache_keys.shape[0]
        me = lax.axis_index("gx")
        z, core = me // 2, lax.rem(me, 2)
        place = jnp.stack([z, core]).astype(jnp.int32)
        gain = norm_gain[None, :]
        inverse_gain = 1.0 / gain
        keyval_padded = jnp.pad(w_keyval, ((0, 0), (0, LANES - kv_cols)))
        news = []
        spread = call(
            spread_kernel,
            jax.ShapeDtypeStruct((gy, own_rows, width), BF16),
            stream,
            gain,
            far=2,
            copies=2,
            buffers=[pltpu.VMEM(stream.shape, F32), pltpu.VMEM(gain.shape, F32)],
        )
        for step in range(STEPS):
            gathered = exchange(spread, "gy").reshape(rows, width)
            packed, squares = call(
                functools.partial(query_kernel, kv_cols),
                (
                    jax.ShapeDtypeStruct((rows, q_cols + LANES), BF16),
                    jax.ShapeDtypeStruct((rows, LANES), BF16),
                ),
                gathered,
                inverse_gain,
                keyval_padded,
                w_query,
            )
            packed = exchange(
                packed.reshape(gx * gy, cache_rows, q_cols + LANES), ("gx", "gy")
            )

            give = hidden_part(place[1:] ^ 1, gathered, w_gate, w_up)
            other = [lax.ppermute(part, "gx", core_swap) for part in (*give, squares)]
            keep = hidden_part(place[1:], gathered, w_gate, w_up)
            pair = call(
                functools.partial(pair_kernel, gz),
                [jax.ShapeDtypeStruct((rows // gz, 2 * half + LANES), BF16)] * gz,
                place,
                *keep,
                squares,
                *other,
                scalars=1,
            )
            arrived = [pair[0]] + [lax.ppermute(pair[n], "gx", z_shift(n)) for n in range(1, gz)]

            packed = lax.optimization_barrier((packed, pair[0]))[0]
            mine = jnp.sum(
                packed.reshape(gx, gy, cache_rows, q_cols + LANES).astype(F32), axis=0
            ).transpose(1, 0, 2)
            at = q_cols + kv_cols
            scale = lax.rsqrt((mine[:, :1, at : at + 1] + mine[:, :1, at + 1 : at + 2]) / D + EPS)
            query = (mine[:, :, :q_cols] * scale).astype(BF16)
            keyval = (mine[:, :, q_cols:at] * scale).astype(BF16).astype(F32)
            news.append(keyval.reshape(cache_rows, 2 * DH))
            attended = attend(lengths, query, news, cache_keys, cache_values)
            blocks = attended.transpose(1, 0, 2)
            blocks = jnp.broadcast_to(blocks[None], (gx, gy, cache_rows, q_cols))
            blocks = blocks.reshape(gx * gy, cache_rows, q_cols)
            heads_all = exchange(blocks, ("gx", "gy")).reshape(rows, q_cols)
            heads_part, held_down = heads_output(heads_all, w_out, w_down)

            arrived = lax.optimization_barrier((arrived, blocks))[0]
            hidden = call(
                functools.partial(hidden_kernel, kv_cols),
                jax.ShapeDtypeStruct((rows // gz, half), BF16),
                *arrived,
            )
            pieces = [hidden] + [lax.ppermute(hidden, "gx", z_shift(n)) for n in range(1, gz)]
            others = [lax.ppermute(piece, "gx", core_swap) for piece in pieces]
            delta = output_part(place, pieces, others, heads_part, held_down)
            delta = exchange(delta.reshape(gy, own_rows, width), "gy")
            stream_shape = jax.ShapeDtypeStruct(stream.shape, F32)
            spread_shape = jax.ShapeDtypeStruct((gy, own_rows, width), BF16)
            if step + 1 < STEPS:
                stream, spread = call(
                    add_kernel, (stream_shape, spread_shape), stream, delta, gain
                )
            else:
                stream = call(add_kernel, stream_shape, stream, delta, gain)
        return stream

    return body


def solution(mesh):
    in_specs = (
        P("gy", "gx"),
        P("gx"),
        P("gx", "gy"),
        P("gx", "gy"),
        P("gx", "gy"),
        P("gx", "gy"),
        P("gy", "gx"),
        P("gy", "gx"),
        P(("gx", "gy"), None, None),
        P(("gx", "gy"), None, None),
        P(("gx", "gy")),
    )
    return jax.shard_map(
        make_body(mesh.shape["gx"], mesh.shape["gy"]),
        mesh=mesh,
        in_specs=in_specs,
        out_specs=P("gy", "gx"),
        check_vma=False,
    )
```

```python
import functools

import jax
import jax.numpy as jnp
from jax import lax
from jax.experimental import pallas as pl
from jax.experimental.pallas import tpu as pltpu
from jax.sharding import PartitionSpec as P

D = 8192
HEADS = 32
DH = 256
STEPS = 2
EPS = 1e-06
LANES = 128
FIRST = 16
F32 = jnp.float32
BF16 = jnp.bfloat16
PARAMS = pltpu.CompilerParams(vmem_limit_bytes=16 * 1024 * 1024)
VMEM = pl.BlockSpec(memory_space=pltpu.VMEM)
SMEM = pl.BlockSpec(memory_space=pltpu.SMEM)
COST = pl.CostEstimate(flops=0, bytes_accessed=0, transcendentals=0)
LATE = pl.CostEstimate(flops=10**10, bytes_accessed=0, transcendentals=0)


def dot32(a, b):
    return jnp.dot(a, b, preferred_element_type=F32)


HBM = pl.BlockSpec(memory_space=pltpu.HBM)


def call(kernel, out_shape, *args, scalars=0, far=0, copies=0, buffers=(), cost=COST):
    near = len(args) - scalars - far
    far_args = [pltpu.with_memory_space_constraint(a, pltpu.HBM) for a in args[scalars + near :]]
    scratch = list(buffers)
    if copies:
        scratch.append(pltpu.SemaphoreType.DMA((copies,)))
    return pl.pallas_call(
        kernel,
        out_shape=out_shape,
        in_specs=[SMEM] * scalars + [VMEM] * near + [HBM] * far,
        scratch_shapes=scratch,
        compiler_params=PARAMS,
        cost_estimate=cost,
    )(*args[: scalars + near], *far_args)


def start_copies(pairs, sems):
    copies = [
        pltpu.make_async_copy(source, target, sems.at[n]) for n, (source, target) in enumerate(pairs)
    ]
    for copy in copies:
        copy.start()
    return copies


def spread_kernel(x_ref, gain_ref, out_ref, x, gain, sems):
    for copy in start_copies([(x_ref, x), (gain_ref, gain)], sems):
        copy.wait()
    scaled = (x[...] * gain[...]).astype(BF16)
    for n in range(out_ref.shape[0]):
        out_ref[n] = scaled


def add_kernel(x_ref, delta_ref, gain_ref, new_ref, out_ref=None):
    new = x_ref[...] + jnp.sum(delta_ref[...].astype(F32), axis=0)
    new_ref[...] = new
    if out_ref is not None:
        scaled = (new * gain_ref[...]).astype(BF16)
        for n in range(out_ref.shape[0]):
            out_ref[n] = scaled


def query_kernel(kv_cols, x_ref, inverse_ref, wkv_ref, wq_ref, out_ref, squares_ref):
    x = x_ref[...]
    plain = x.astype(F32) * inverse_ref[...]
    squares = jnp.sum(plain * plain, axis=1, keepdims=True)
    high = squares.astype(BF16).astype(F32)
    low = squares - high
    lane = lax.broadcasted_iota(jnp.int32, squares_ref.shape, 1)
    columns = jnp.where(lane == kv_cols, high, jnp.where(lane == kv_cols + 1, low, 0.0))
    squares_ref[...] = columns.astype(BF16)
    q_cols = wq_ref.shape[1]
    out_ref[:, :q_cols] = dot32(x, wq_ref[...]).astype(BF16)
    out_ref[:, q_cols:] = (dot32(x, wkv_ref[...]) + columns).astype(BF16)


def hidden_part_kernel(half_ref, x_ref, wg_ref, wu_ref, *outs):
    block = wg_ref.shape[1]
    wide = outs[0].shape[1]
    for n in range(len(outs) // 2 * (wide // block)):

        @pl.when(pl.program_id(0) == n)
        def _():
            at = n * block
            for k, ref in enumerate((wg_ref, wu_ref)):
                outs[at // wide * 2 + k][:, at % wide : at % wide + block] = dot32(
                    x_ref[...], ref[...]
                ).astype(BF16)


def hidden_part(half_index, x, w_gate, w_up, outs=2, blocks=2):
    rows, width = x.shape
    half = w_gate.shape[1] // 2
    weight = pl.BlockSpec((width, half // blocks), lambda n, h: (0, h[0] * blocks + n))
    part = jax.ShapeDtypeStruct((rows, half // outs), BF16)
    return pl.pallas_call(
        hidden_part_kernel,
        out_shape=[part] * (2 * outs),
        grid_spec=pltpu.PrefetchScalarGridSpec(
            num_scalar_prefetch=1,
            grid=(blocks,),
            in_specs=[pl.BlockSpec(x.shape, lambda n, h: (0, 0)), weight, weight],
            out_specs=[pl.BlockSpec(part.shape, lambda n, h: (0, 0))] * (2 * outs),
        ),
        compiler_params=PARAMS,
        cost_estimate=COST,
    )(
        half_index,
        x,
        pltpu.with_memory_space_constraint(w_gate, pltpu.HBM),
        pltpu.with_memory_space_constraint(w_up, pltpu.HBM),
    )


def pair_kernel(gz, z_ref, *refs):
    outs = refs[-gz:]
    count = (len(refs) - gz) // 2
    half = sum(ref.shape[1] for ref in refs[: count - 1]) // 2
    size = outs[0].shape[0]
    for n in range(gz):
        here = pl.ds(pl.multiple_of(lax.rem(z_ref[0] + n, gz) * size, size), size)
        for k in range(count):
            keep, other = refs[k], refs[count + k]
            block = keep.shape[1]
            at = 2 * half if k == count - 1 else k % 2 * half + k // 2 * block
            outs[n][:, at : at + block] = (
                keep[here, :].astype(F32) + other[here, :].astype(F32)
            ).astype(BF16)


def hidden_kernel(kv_cols, *refs):
    out_ref = refs[-1]
    half = out_ref.shape[1]
    total = refs[0][...].astype(F32)
    for ref in refs[1:-1]:
        total = total + ref[...].astype(F32)
    at = 2 * half + kv_cols
    scale = lax.rsqrt((total[:, at : at + 1] + total[:, at + 1 : at + 2]) / D + EPS)
    gate = total[:, :half] * scale
    up = total[:, half : 2 * half] * scale
    out_ref[...] = (gate / (1.0 + jnp.exp(-gate)) * up).astype(BF16)


def attend_kernel(steps, kv_cols, lengths_ref, sums_ref, raw_ref, *refs):
    news = refs[: steps - 1]
    keys_ref, values_ref, out_ref, fresh_ref, keys, values, sems = refs[steps - 1 :]
    rows, count = sums_ref.shape[:2]
    q_cols = sums_ref.shape[2] - LANES
    first = pl.ds(0, FIRST)
    rest = pl.ds(FIRST, keys.shape[1] - FIRST)
    spots = [(0, first), (0, rest)] + [(row, pl.ds(0, keys.shape[1])) for row in range(1, rows)]
    key_copies = start_copies(
        [(keys_ref.at[row, at], keys.at[row, at]) for row, at in spots], sems.at[: rows + 1]
    )
    key_copies[0].wait()
    value_copies = start_copies(
        [(values_ref.at[row], values.at[row]) for row in range(rows)], sems.at[rows + 1 :]
    )
    scale = DH**-0.5
    heads, scores, new_scores, new_values = [], [], [], []
    for row in range(rows):
        at = q_cols + kv_cols
        line = sums_ref[row, 0:1, :]
        row_scale = lax.rsqrt((line[:, at : at + 1] + line[:, at + 1 : at + 2]) / D + EPS)
        q = (sums_ref[row, :, :q_cols] * row_scale).astype(BF16)
        fresh = (raw_ref[row : row + 1, :] * row_scale).astype(BF16).astype(F32)
        fresh_ref[row : row + 1, :] = fresh
        heads.append(jnp.concatenate([q[:, :DH], q[:, DH:]], axis=0))
        heads32 = heads[row].astype(F32)
        lines = [ref[row : row + 1, :] for ref in news] + [fresh]
        new_scores.append(
            [jnp.sum(heads32 * line[:, :DH], axis=1, keepdims=True) * scale for line in lines]
        )
        new_values.append([line[:, DH:] for line in lines])
    for copy in key_copies[1:]:
        copy.wait()
    for row in range(rows):
        old_s = lax.dot_general(
            heads[row], keys[row], (((1,), (1,)), ((), ())), preferred_element_type=F32
        )
        place = lax.broadcasted_iota(jnp.int32, old_s.shape, 1)
        scores.append(jnp.where(place < lengths_ref[row], old_s * scale, -jnp.inf))
    weights = []
    for row in range(rows):
        top = jnp.max(scores[row], axis=1, keepdims=True)
        for score in new_scores[row]:
            top = jnp.maximum(top, score)
        old_e = jnp.exp(scores[row] - top)
        new_e = [jnp.exp(score - top) for score in new_scores[row]]
        total = jnp.sum(old_e, axis=1, keepdims=True)
        for e in new_e:
            total = total + e
        share = 1.0 / total
        weights.append(((old_e * share).astype(BF16), [(e * share).astype(BF16) for e in new_e]))
    for copy in value_copies:
        copy.wait()
    for row in range(rows):
        old_w, new_w = weights[row]
        result = dot32(old_w, values[row])
        for w, v in zip(new_w, new_values[row]):
            result = result + w.astype(F32) * v
        out_ref[row] = jnp.concatenate([result[:count], result[count:]], axis=1).astype(BF16)


def attend(lengths, sums, raw, news, keys, values, kv_cols):
    rows, blocks, cols = sums.shape
    return call(
        functools.partial(attend_kernel, len(news) + 1, kv_cols),
        [
            jax.ShapeDtypeStruct((rows, blocks, cols - LANES), BF16),
            jax.ShapeDtypeStruct(raw.shape, F32),
        ],
        lengths,
        sums,
        raw,
        *news,
        keys,
        values,
        scalars=1,
        far=2,
        copies=2 * rows + 1,
        buffers=[pltpu.VMEM(keys.shape, BF16), pltpu.VMEM(values.shape, BF16)],
    )


def heads_kernel(blocks, heads_ref, wout_ref, down_ref, out_ref, held_ref, buffer, sems):
    width = out_ref.shape[1]
    block = width // blocks
    spots = [pl.ds(at, block) for at in range(0, width, block)]
    pairs = [(wout_ref.at[:, spot], buffer.at[:, spot]) for spot in spots]
    pairs += [(down_ref.at[:, spot], held_ref.at[:, spot]) for spot in spots]
    copies = start_copies(pairs, sems)
    for n, spot in enumerate(spots):
        copies[n].wait()
        out_ref[:, spot] = dot32(heads_ref[...], buffer[:, spot])
    for copy in copies[blocks:]:
        copy.wait()


def heads_output(heads, w_out, w_down, blocks=4):
    width = w_out.shape[1]
    return call(
        functools.partial(heads_kernel, blocks),
        [
            jax.ShapeDtypeStruct((heads.shape[0], width), F32),
            pltpu.VMEM(w_down.shape, w_down.dtype),
        ],
        heads,
        w_out,
        w_down,
        far=2,
        copies=2 * blocks,
        buffers=[pltpu.VMEM(w_out.shape, BF16)],
        cost=LATE,
    )


def output_kernel(gz, block, place_ref, *refs):
    pieces, others = refs[:gz], refs[gz : 2 * gz]
    heads_ref, down_ref, out_ref, hidden = refs[2 * gz :]
    size, half = pieces[0].shape
    z, c = place_ref[0], place_ref[1]
    mine = pl.ds(pl.multiple_of(c * half, half), half)
    theirs = pl.ds(pl.multiple_of((1 - c) * half, half), half)
    for n in range(gz):
        at = pl.ds(pl.multiple_of(lax.rem(z + gz - n, gz) * size, size), size)
        hidden[at, mine] = pieces[n][...]
        hidden[at, theirs] = others[n][...]
    for at in range(0, out_ref.shape[1], block):
        out_ref[:, at : at + block] = (
            dot32(hidden[...], down_ref[:, at : at + block]) + heads_ref[:, at : at + block]
        ).astype(BF16)


def output_part(place, pieces, others, heads_part, w_down):
    return call(
        functools.partial(output_kernel, len(pieces), 512),
        jax.ShapeDtypeStruct(heads_part.shape, BF16),
        place,
        *pieces,
        *others,
        heads_part,
        w_down,
        scalars=1,
        buffers=[pltpu.VMEM((heads_part.shape[0], w_down.shape[0]), BF16)],
    )


def make_body(gx, gy):
    gz = gx // 2
    core_swap = [(n, n ^ 1) for n in range(gx)]

    def z_shift(n):
        return [(2 * z + c, 2 * ((z + n) % gz) + c) for z in range(gz) for c in range(2)]

    def exchange(parts, axis):
        return lax.all_to_all(parts, axis, split_axis=0, concat_axis=0, tiled=False)

    def body(
        residual,
        norm_gain,
        w_gate,
        w_up,
        w_query,
        w_keyval,
        w_down,
        w_out,
        cache_keys,
        cache_values,
        lengths,
    ):
        stream = residual
        own_rows, width = residual.shape
        rows = own_rows * gy
        half = w_gate.shape[1] // 2
        q_cols = w_query.shape[1]
        kv_cols = w_keyval.shape[1]
        cache_rows = cache_keys.shape[0]
        me = lax.axis_index("gx")
        z, core = me // 2, lax.rem(me, 2)
        place = jnp.stack([z, core]).astype(jnp.int32)
        gain = norm_gain[None, :]
        inverse_gain = 1.0 / gain
        keyval_padded = jnp.pad(w_keyval, ((0, 0), (0, LANES - kv_cols)))
        news = []
        spread = call(
            spread_kernel,
            jax.ShapeDtypeStruct((gy, own_rows, width), BF16),
            stream,
            gain,
            far=2,
            copies=2,
            buffers=[pltpu.VMEM(stream.shape, F32), pltpu.VMEM(gain.shape, F32)],
        )
        for step in range(STEPS):
            gathered = exchange(spread, "gy").reshape(rows, width)
            packed, squares = call(
                functools.partial(query_kernel, kv_cols),
                (
                    jax.ShapeDtypeStruct((rows, q_cols + LANES), BF16),
                    jax.ShapeDtypeStruct((rows, LANES), BF16),
                ),
                gathered,
                inverse_gain,
                keyval_padded,
                w_query,
            )
            packed = exchange(
                packed.reshape(gx * gy, cache_rows, q_cols + LANES), ("gx", "gy")
            )

            give = hidden_part(place[1:] ^ 1, gathered, w_gate, w_up)
            other = [lax.ppermute(part, "gx", core_swap) for part in (*give, squares)]
            keep = hidden_part(place[1:], gathered, w_gate, w_up)
            pair = call(
                functools.partial(pair_kernel, gz),
                [jax.ShapeDtypeStruct((rows // gz, 2 * half + LANES), BF16)] * gz,
                place,
                *keep,
                squares,
                *other,
                scalars=1,
            )
            arrived = [pair[0]] + [lax.ppermute(pair[n], "gx", z_shift(n)) for n in range(1, gz)]

            packed = lax.optimization_barrier((packed, pair[0]))[0]
            mine = jnp.sum(
                packed.reshape(gx, gy, cache_rows, q_cols + LANES).astype(F32), axis=0
            ).transpose(1, 0, 2)
            at = q_cols + kv_cols
            raw = mine[:, :, q_cols:at].reshape(cache_rows, 2 * DH)
            attended, fresh = attend(
                lengths, mine, raw, news, cache_keys, cache_values, kv_cols
            )
            news.append(fresh)
            blocks = attended.transpose(1, 0, 2)
            blocks = jnp.broadcast_to(blocks[None], (gx, gy, cache_rows, q_cols))
            blocks = blocks.reshape(gx * gy, cache_rows, q_cols)
            heads_all = exchange(blocks, ("gx", "gy")).reshape(rows, q_cols)
            arrived = lax.optimization_barrier((arrived, blocks))[0]
            hidden = call(
                functools.partial(hidden_kernel, kv_cols),
                jax.ShapeDtypeStruct((rows // gz, half), BF16),
                *arrived,
            )
            pieces = [hidden] + [lax.ppermute(hidden, "gx", z_shift(n)) for n in range(1, gz)]
            own_other = lax.ppermute(hidden, "gx", core_swap)
            heads_all = lax.optimization_barrier((heads_all, own_other))[0]
            heads_part, held_down = heads_output(heads_all, w_out, w_down)
            late = lax.optimization_barrier((pieces[1:], heads_part))[0]
            others = [own_other] + [lax.ppermute(piece, "gx", core_swap) for piece in late]
            delta = output_part(place, pieces, others, heads_part, held_down)
            delta = exchange(delta.reshape(gy, own_rows, width), "gy")
            stream_shape = jax.ShapeDtypeStruct(stream.shape, F32)
            spread_shape = jax.ShapeDtypeStruct((gy, own_rows, width), BF16)
            if step + 1 < STEPS:
                stream, spread = call(
                    add_kernel, (stream_shape, spread_shape), stream, delta, gain
                )
            else:
                stream = call(add_kernel, stream_shape, stream, delta, gain)
        return stream

    return body


def solution(mesh):
    in_specs = (
        P("gy", "gx"),
        P("gx"),
        P("gx", "gy"),
        P("gx", "gy"),
        P("gx", "gy"),
        P("gx", "gy"),
        P("gy", "gx"),
        P("gy", "gx"),
        P(("gx", "gy"), None, None),
        P(("gx", "gy"), None, None),
        P(("gx", "gy")),
    )
    return jax.shard_map(
        make_body(mesh.shape["gx"], mesh.shape["gy"]),
        mesh=mesh,
        in_specs=in_specs,
        out_specs=P("gy", "gx"),
        check_vma=False,
    )
```

```python
import functools

import jax
import jax.numpy as jnp
from jax import lax
from jax.experimental import pallas as pl
from jax.experimental.pallas import tpu as pltpu
from jax.sharding import PartitionSpec as P

D = 8192
HEADS = 32
DH = 256
STEPS = 2
EPS = 1e-06
LANES = 128
FIRST = 16
F32 = jnp.float32
BF16 = jnp.bfloat16
PARAMS = pltpu.CompilerParams(vmem_limit_bytes=16 * 1024 * 1024)
VMEM = pl.BlockSpec(memory_space=pltpu.VMEM)
SMEM = pl.BlockSpec(memory_space=pltpu.SMEM)
COST = pl.CostEstimate(flops=0, bytes_accessed=0, transcendentals=0)
LATE = pl.CostEstimate(flops=10**10, bytes_accessed=0, transcendentals=0)


def dot32(a, b):
    return jnp.dot(a, b, preferred_element_type=F32)


HBM = pl.BlockSpec(memory_space=pltpu.HBM)


def call(kernel, out_shape, *args, scalars=0, far=0, copies=0, buffers=(), cost=COST):
    near = len(args) - scalars - far
    far_args = [pltpu.with_memory_space_constraint(a, pltpu.HBM) for a in args[scalars + near :]]
    scratch = list(buffers)
    if copies:
        scratch.append(pltpu.SemaphoreType.DMA((copies,)))
    return pl.pallas_call(
        kernel,
        out_shape=out_shape,
        in_specs=[SMEM] * scalars + [VMEM] * near + [HBM] * far,
        scratch_shapes=scratch,
        compiler_params=PARAMS,
        cost_estimate=cost,
    )(*args[: scalars + near], *far_args)


def start_copies(pairs, sems):
    copies = [
        pltpu.make_async_copy(source, target, sems.at[n]) for n, (source, target) in enumerate(pairs)
    ]
    for copy in copies:
        copy.start()
    return copies


def spread_kernel(x_ref, gain_ref, out_ref, x, gain, sems):
    for copy in start_copies([(x_ref, x), (gain_ref, gain)], sems):
        copy.wait()
    scaled = (x[...] * gain[...]).astype(BF16)
    for n in range(out_ref.shape[0]):
        out_ref[n] = scaled


def add_kernel(x_ref, delta_ref, gain_ref, new_ref, out_ref=None):
    new = x_ref[...] + jnp.sum(delta_ref[...].astype(F32), axis=0)
    new_ref[...] = new
    if out_ref is not None:
        scaled = (new * gain_ref[...]).astype(BF16)
        for n in range(out_ref.shape[0]):
            out_ref[n] = scaled


def query_kernel(x_ref, gain_ref, wkv_ref, wq_ref, out_ref, squares_ref):
    x = x_ref[...]
    kv_cols, depth = wkv_ref.shape
    plain = x.astype(F32) * (1.0 / gain_ref[...])
    squares = jnp.sum(plain * plain, axis=1, keepdims=True)
    high = squares.astype(BF16).astype(F32)
    low = squares - high
    lane = lax.broadcasted_iota(jnp.int32, squares_ref.shape, 1)
    columns = jnp.where(lane == kv_cols, high, jnp.where(lane == kv_cols + 1, low, 0.0))
    squares_ref[...] = columns.astype(BF16)
    q_cols = wq_ref.shape[1]
    out_ref[:, :q_cols] = dot32(x, wq_ref[...]).astype(BF16)
    wkv = jnp.concatenate([wkv_ref[...], jnp.zeros((LANES - kv_cols, depth), BF16)], axis=0)
    keyval = lax.dot_general(x, wkv, (((1,), (1,)), ((), ())), preferred_element_type=F32)
    out_ref[:, q_cols:] = (keyval + columns).astype(BF16)


def hidden_part_kernel(half_ref, x_ref, wg_ref, wu_ref, *outs):
    half = wg_ref.shape[1] // 2
    block = outs[0].shape[1]
    start = half_ref[0] * half
    for n in range(len(outs) // 2):
        here = pl.ds(pl.multiple_of(start + n * block, block), block)
        outs[2 * n][...] = dot32(x_ref[...], wg_ref[:, here]).astype(BF16)
        outs[2 * n + 1][...] = dot32(x_ref[...], wu_ref[:, here]).astype(BF16)


def hidden_part(half_index, x, w_gate, w_up, blocks=2):
    part = jax.ShapeDtypeStruct((x.shape[0], w_gate.shape[1] // 2 // blocks), BF16)
    return call(
        hidden_part_kernel, [part] * (2 * blocks), half_index, x, w_gate, w_up, scalars=1
    )


def pair_kernel(gz, z_ref, *refs):
    outs = refs[-gz:]
    count = (len(refs) - gz) // 2
    half = sum(ref.shape[1] for ref in refs[: count - 1]) // 2
    size = outs[0].shape[0]
    for n in range(gz):
        here = pl.ds(pl.multiple_of(lax.rem(z_ref[0] + n, gz) * size, size), size)
        for k in range(count):
            keep, other = refs[k], refs[count + k]
            block = keep.shape[1]
            at = 2 * half if k == count - 1 else k % 2 * half + k // 2 * block
            outs[n][:, at : at + block] = (
                keep[here, :].astype(F32) + other[here, :].astype(F32)
            ).astype(BF16)


def hidden_kernel(kv_cols, *refs):
    out_ref = refs[-1]
    half = out_ref.shape[1]
    total = refs[0][...].astype(F32)
    for ref in refs[1:-1]:
        total = total + ref[...].astype(F32)
    at = 2 * half + kv_cols
    scale = lax.rsqrt((total[:, at : at + 1] + total[:, at + 1 : at + 2]) / D + EPS)
    gate = total[:, :half] * scale
    up = total[:, half : 2 * half] * scale
    out_ref[...] = (gate / (1.0 + jnp.exp(-gate)) * up).astype(BF16)


def attend_kernel(steps, kv_cols, lengths_ref, sums_ref, raw_ref, *refs):
    news = refs[: steps - 1]
    keys_ref, values_ref, out_ref, fresh_ref, keys, values, sems = refs[steps - 1 :]
    rows, count = sums_ref.shape[:2]
    q_cols = sums_ref.shape[2] - LANES
    first = pl.ds(0, FIRST)
    rest = pl.ds(FIRST, keys.shape[1] - FIRST)
    spots = [(0, first), (0, rest)] + [(row, pl.ds(0, keys.shape[1])) for row in range(1, rows)]
    key_copies = start_copies(
        [(keys_ref.at[row, at], keys.at[row, at]) for row, at in spots], sems.at[: rows + 1]
    )
    key_copies[0].wait()
    value_copies = start_copies(
        [(values_ref.at[row], values.at[row]) for row in range(rows)], sems.at[rows + 1 :]
    )
    scale = DH**-0.5
    heads, scores, new_scores, new_values = [], [], [], []
    for row in range(rows):
        at = q_cols + kv_cols
        line = sums_ref[row, 0:1, :]
        row_scale = lax.rsqrt((line[:, at : at + 1] + line[:, at + 1 : at + 2]) / D + EPS)
        q = (sums_ref[row, :, :q_cols] * row_scale).astype(BF16)
        fresh = (raw_ref[row : row + 1, :] * row_scale).astype(BF16).astype(F32)
        fresh_ref[row : row + 1, :] = fresh
        heads.append(jnp.concatenate([q[:, :DH], q[:, DH:]], axis=0))
        heads32 = heads[row].astype(F32)
        lines = [ref[row : row + 1, :] for ref in news] + [fresh]
        new_scores.append(
            [jnp.sum(heads32 * line[:, :DH], axis=1, keepdims=True) * scale for line in lines]
        )
        new_values.append([line[:, DH:] for line in lines])
    for copy in key_copies[1:]:
        copy.wait()
    for row in range(rows):
        old_s = lax.dot_general(
            heads[row], keys[row], (((1,), (1,)), ((), ())), preferred_element_type=F32
        )
        place = lax.broadcasted_iota(jnp.int32, old_s.shape, 1)
        scores.append(jnp.where(place < lengths_ref[row], old_s * scale, -jnp.inf))
    weights = []
    for row in range(rows):
        top = jnp.max(scores[row], axis=1, keepdims=True)
        for score in new_scores[row]:
            top = jnp.maximum(top, score)
        old_e = jnp.exp(scores[row] - top)
        new_e = [jnp.exp(score - top) for score in new_scores[row]]
        total = jnp.sum(old_e, axis=1, keepdims=True)
        for e in new_e:
            total = total + e
        share = 1.0 / total
        weights.append(((old_e * share).astype(BF16), [(e * share).astype(BF16) for e in new_e]))
    for copy in value_copies:
        copy.wait()
    for row in range(rows):
        old_w, new_w = weights[row]
        result = dot32(old_w, values[row])
        for w, v in zip(new_w, new_values[row]):
            result = result + w.astype(F32) * v
        out_ref[row] = jnp.concatenate([result[:count], result[count:]], axis=1).astype(BF16)


def attend(lengths, sums, raw, news, keys, values, kv_cols):
    rows, blocks, cols = sums.shape
    return call(
        functools.partial(attend_kernel, len(news) + 1, kv_cols),
        [
            jax.ShapeDtypeStruct((rows, blocks, cols - LANES), BF16),
            jax.ShapeDtypeStruct(raw.shape, F32),
        ],
        lengths,
        sums,
        raw,
        *news,
        keys,
        values,
        scalars=1,
        far=2,
        copies=2 * rows + 1,
        buffers=[pltpu.VMEM(keys.shape, BF16), pltpu.VMEM(values.shape, BF16)],
    )


def heads_kernel(blocks, heads_ref, wout_ref, down_ref, out_ref, held_ref, buffer, sems):
    width = out_ref.shape[1]
    block = width // blocks
    spots = [pl.ds(at, block) for at in range(0, width, block)]
    pairs = [(wout_ref.at[:, spot], buffer.at[:, spot]) for spot in spots]
    pairs += [(down_ref.at[:, spot], held_ref.at[:, spot]) for spot in spots]
    copies = start_copies(pairs, sems)
    for n, spot in enumerate(spots):
        copies[n].wait()
        out_ref[:, spot] = dot32(heads_ref[...], buffer[:, spot])
    for copy in copies[blocks:]:
        copy.wait()


def heads_output(heads, w_out, w_down, blocks=4):
    width = w_out.shape[1]
    return call(
        functools.partial(heads_kernel, blocks),
        [
            jax.ShapeDtypeStruct((heads.shape[0], width), F32),
            pltpu.VMEM(w_down.shape, w_down.dtype),
        ],
        heads,
        w_out,
        w_down,
        far=2,
        copies=2 * blocks,
        buffers=[pltpu.VMEM(w_out.shape, BF16)],
        cost=LATE,
    )


def output_kernel(gz, block, core_flip, place_ref, *refs):
    pieces = refs[:gz]
    part_ref, down_ref, out_ref, hidden = refs[gz:]
    size, half = pieces[0].shape
    z = place_ref[0]
    core = 1 - place_ref[1] if core_flip else place_ref[1]
    here = pl.ds(pl.multiple_of(core * half, half), half)
    for n in range(gz):
        at = pl.ds(pl.multiple_of(lax.rem(z + gz - n, gz) * size, size), size)
        hidden[at, :] = pieces[n][...]
    for at in range(0, out_ref.shape[1], block):
        out_ref[:, at : at + block] = (
            dot32(hidden[...], down_ref[here, at : at + block]) + part_ref[:, at : at + block]
        ).astype(out_ref.dtype)


def output_part(place, pieces, part, w_down, core_flip, dtype):
    return call(
        functools.partial(output_kernel, len(pieces), 512, core_flip),
        jax.ShapeDtypeStruct(part.shape, dtype),
        place,
        *pieces,
        part,
        w_down,
        scalars=1,
        buffers=[pltpu.VMEM((part.shape[0], w_down.shape[0] // 2), BF16)],
    )


def make_body(gx, gy):
    gz = gx // 2
    core_swap = [(n, n ^ 1) for n in range(gx)]

    def z_shift(n):
        return [(2 * z + c, 2 * ((z + n) % gz) + c) for z in range(gz) for c in range(2)]

    def exchange(parts, axis):
        return lax.all_to_all(parts, axis, split_axis=0, concat_axis=0, tiled=False)

    def body(
        residual,
        norm_gain,
        w_gate,
        w_up,
        w_query,
        w_keyval,
        w_down,
        w_out,
        cache_keys,
        cache_values,
        lengths,
    ):
        own_rows, width = residual.shape
        rows = own_rows * gy
        half = w_gate.shape[1] // 2
        q_cols = w_query.shape[1]
        kv_cols = w_keyval.shape[1]
        cache_rows = cache_keys.shape[0]
        me = lax.axis_index("gx")
        z, core = me // 2, lax.rem(me, 2)
        place = jnp.stack([z, core]).astype(jnp.int32)
        stream, place, mine_half, other_half = lax.optimization_barrier(
            (residual, place, place[1:], place[1:] ^ 1)
        )
        gain = norm_gain[None, :]
        news = []
        spread = call(
            spread_kernel,
            jax.ShapeDtypeStruct((gy, own_rows, width), BF16),
            stream,
            gain,
            far=2,
            copies=2,
            buffers=[pltpu.VMEM(stream.shape, F32), pltpu.VMEM(gain.shape, F32)],
            cost=LATE,
        )
        for step in range(STEPS):
            gathered = exchange(spread, "gy").reshape(rows, width)
            packed, squares = call(
                query_kernel,
                (
                    jax.ShapeDtypeStruct((rows, q_cols + LANES), BF16),
                    jax.ShapeDtypeStruct((rows, LANES), BF16),
                ),
                gathered,
                gain,
                w_keyval.T,
                w_query,
            )
            give = hidden_part(other_half, gathered, w_gate, w_up)
            other = [lax.ppermute(part, "gx", core_swap) for part in (*give, squares)]
            keep = hidden_part(mine_half, gathered, w_gate, w_up)
            packed = lax.optimization_barrier((packed, give, keep))[0]
            packed = exchange(
                packed.reshape(gx * gy, cache_rows, q_cols + LANES), ("gx", "gy")
            )
            pair = call(
                functools.partial(pair_kernel, gz),
                [jax.ShapeDtypeStruct((rows // gz, 2 * half + LANES), BF16)] * gz,
                place,
                *keep,
                squares,
                *other,
                scalars=1,
            )
            arrived = [pair[0]] + [lax.ppermute(pair[n], "gx", z_shift(n)) for n in range(1, gz)]

            packed = lax.optimization_barrier((packed, pair[0]))[0]
            mine = jnp.sum(
                packed.reshape(gx, gy, cache_rows, q_cols + LANES).astype(F32), axis=0
            ).transpose(1, 0, 2)
            at = q_cols + kv_cols
            raw = mine[:, :, q_cols:at].reshape(cache_rows, 2 * DH)
            attended, fresh = attend(
                lengths, mine, raw, news, cache_keys, cache_values, kv_cols
            )
            news.append(fresh)
            blocks = attended.transpose(1, 0, 2)
            blocks = jnp.broadcast_to(blocks[None], (gx, gy, cache_rows, q_cols))
            blocks = blocks.reshape(gx * gy, cache_rows, q_cols)
            heads_all = exchange(blocks, ("gx", "gy")).reshape(rows, q_cols)
            arrived = lax.optimization_barrier((arrived, blocks))[0]
            hidden = call(
                functools.partial(hidden_kernel, kv_cols),
                jax.ShapeDtypeStruct((rows // gz, half), BF16),
                *arrived,
            )
            pieces = [hidden] + [lax.ppermute(hidden, "gx", z_shift(n)) for n in range(1, gz)]
            own_other = lax.ppermute(hidden, "gx", core_swap)
            heads_all = lax.optimization_barrier((heads_all, own_other))[0]
            heads_part, held_down = heads_output(heads_all, w_out, w_down)
            late = lax.optimization_barrier((pieces[1:], heads_part))[0]
            others = [own_other] + [lax.ppermute(piece, "gx", core_swap) for piece in late]
            part = output_part(place, pieces, heads_part, held_down, False, F32)
            delta = output_part(place, others, part, held_down, True, BF16)
            delta = exchange(delta.reshape(gy, own_rows, width), "gy")
            stream_shape = jax.ShapeDtypeStruct(stream.shape, F32)
            spread_shape = jax.ShapeDtypeStruct((gy, own_rows, width), BF16)
            if step + 1 < STEPS:
                stream, spread = call(
                    add_kernel, (stream_shape, spread_shape), stream, delta, gain
                )
            else:
                stream = call(add_kernel, stream_shape, stream, delta, gain)
        return stream

    return body


def solution(mesh):
    in_specs = (
        P("gy", "gx"),
        P("gx"),
        P("gx", "gy"),
        P("gx", "gy"),
        P("gx", "gy"),
        P("gx", "gy"),
        P("gy", "gx"),
        P("gy", "gx"),
        P(("gx", "gy"), None, None),
        P(("gx", "gy"), None, None),
        P(("gx", "gy")),
    )
    return jax.shard_map(
        make_body(mesh.shape["gx"], mesh.shape["gy"]),
        mesh=mesh,
        in_specs=in_specs,
        out_specs=P("gy", "gx"),
        check_vma=False,
    )
```

```python
import functools

import jax
import jax.numpy as jnp
from jax import lax
from jax.experimental import pallas as pl
from jax.experimental.pallas import tpu as pltpu
from jax.sharding import PartitionSpec as P

D = 8192
HEADS = 32
DH = 256
STEPS = 2
EPS = 1e-06
LANES = 128
FIRST = 16
F32 = jnp.float32
BF16 = jnp.bfloat16
PARAMS = pltpu.CompilerParams(vmem_limit_bytes=16 * 1024 * 1024)
VMEM = pl.BlockSpec(memory_space=pltpu.VMEM)
SMEM = pl.BlockSpec(memory_space=pltpu.SMEM)
COST = pl.CostEstimate(flops=0, bytes_accessed=0, transcendentals=0)
LATE = pl.CostEstimate(flops=10**10, bytes_accessed=0, transcendentals=0)


def dot32(a, b):
    return jnp.dot(a, b, preferred_element_type=F32)


HBM = pl.BlockSpec(memory_space=pltpu.HBM)


def call(kernel, out_shape, *args, scalars=0, far=0, copies=0, buffers=(), cost=COST):
    near = len(args) - scalars - far
    far_args = [pltpu.with_memory_space_constraint(a, pltpu.HBM) for a in args[scalars + near :]]
    scratch = list(buffers)
    if copies:
        scratch.append(pltpu.SemaphoreType.DMA((copies,)))
    return pl.pallas_call(
        kernel,
        out_shape=out_shape,
        in_specs=[SMEM] * scalars + [VMEM] * near + [HBM] * far,
        scratch_shapes=scratch,
        compiler_params=PARAMS,
        cost_estimate=cost,
    )(*args[: scalars + near], *far_args)


def start_copies(pairs, sems):
    copies = [
        pltpu.make_async_copy(source, target, sems.at[n]) for n, (source, target) in enumerate(pairs)
    ]
    for copy in copies:
        copy.start()
    return copies


def spread_kernel(x_ref, gain_ref, wq_ref, out_ref, held_ref, x, gain, sems):
    copies = start_copies([(x_ref, x), (gain_ref, gain), (wq_ref, held_ref)], sems)
    copies[0].wait()
    copies[1].wait()
    scaled = (x[...] * gain[...]).astype(BF16)
    for n in range(out_ref.shape[0]):
        out_ref[n] = scaled
    copies[2].wait()


def add_kernel(x_ref, delta_ref, gain_ref, new_ref, out_ref=None):
    new = x_ref[...] + jnp.sum(delta_ref[...].astype(F32), axis=0)
    new_ref[...] = new
    if out_ref is not None:
        scaled = (new * gain_ref[...]).astype(BF16)
        for n in range(out_ref.shape[0]):
            out_ref[n] = scaled


def query_kernel(x_ref, gain_ref, wkv_ref, wq_ref, out_ref, squares_ref):
    x = x_ref[...]
    kv_cols, depth = wkv_ref.shape
    plain = x.astype(F32) * (1.0 / gain_ref[...])
    squares = jnp.sum(plain * plain, axis=1, keepdims=True)
    high = squares.astype(BF16).astype(F32)
    low = squares - high
    lane = lax.broadcasted_iota(jnp.int32, squares_ref.shape, 1)
    columns = jnp.where(lane == kv_cols, high, jnp.where(lane == kv_cols + 1, low, 0.0))
    squares_ref[...] = columns.astype(BF16)
    q_cols = wq_ref.shape[1]
    out_ref[:, :q_cols] = dot32(x, wq_ref[...]).astype(BF16)
    wkv = jnp.concatenate([wkv_ref[...], jnp.zeros((LANES - kv_cols, depth), BF16)], axis=0)
    keyval = lax.dot_general(x, wkv, (((1,), (1,)), ((), ())), preferred_element_type=F32)
    out_ref[:, q_cols:] = (keyval + columns).astype(BF16)


def hidden_part_kernel(half_ref, x_ref, wg_ref, wu_ref, *outs):
    half = wg_ref.shape[1] // 2
    block = outs[0].shape[1]
    start = half_ref[0] * half
    for n in range(len(outs) // 2):
        here = pl.ds(pl.multiple_of(start + n * block, block), block)
        outs[2 * n][...] = dot32(x_ref[...], wg_ref[:, here]).astype(BF16)
        outs[2 * n + 1][...] = dot32(x_ref[...], wu_ref[:, here]).astype(BF16)


def hidden_part(half_index, x, w_gate, w_up, blocks=2):
    part = jax.ShapeDtypeStruct((x.shape[0], w_gate.shape[1] // 2 // blocks), BF16)
    return call(
        hidden_part_kernel, [part] * (2 * blocks), half_index, x, w_gate, w_up, scalars=1
    )


def pair_kernel(gz, z_ref, *refs):
    outs = refs[-gz:]
    count = (len(refs) - gz) // 2
    half = sum(ref.shape[1] for ref in refs[: count - 1]) // 2
    size = outs[0].shape[0]
    for n in range(gz):
        here = pl.ds(pl.multiple_of(lax.rem(z_ref[0] + n, gz) * size, size), size)
        for k in range(count):
            keep, other = refs[k], refs[count + k]
            block = keep.shape[1]
            at = 2 * half if k == count - 1 else k % 2 * half + k // 2 * block
            outs[n][:, at : at + block] = (
                keep[here, :].astype(F32) + other[here, :].astype(F32)
            ).astype(BF16)


def hidden_kernel(kv_cols, *refs):
    out_ref = refs[-1]
    half = out_ref.shape[1]
    total = refs[0][...].astype(F32)
    for ref in refs[1:-1]:
        total = total + ref[...].astype(F32)
    at = 2 * half + kv_cols
    scale = lax.rsqrt((total[:, at : at + 1] + total[:, at + 1 : at + 2]) / D + EPS)
    gate = total[:, :half] * scale
    up = total[:, half : 2 * half] * scale
    out_ref[...] = (gate / (1.0 + jnp.exp(-gate)) * up).astype(BF16)


def attend_kernel(steps, kv_cols, lengths_ref, sums_ref, raw_ref, *refs):
    news = refs[: steps - 1]
    keys_ref, values_ref, out_ref, fresh_ref, keys, values, sems = refs[steps - 1 :]
    rows, count = sums_ref.shape[:2]
    q_cols = sums_ref.shape[2] - LANES
    first = pl.ds(0, FIRST)
    rest = pl.ds(FIRST, keys.shape[1] - FIRST)
    spots = [(0, first), (0, rest)] + [(row, pl.ds(0, keys.shape[1])) for row in range(1, rows)]
    key_copies = start_copies(
        [(keys_ref.at[row, at], keys.at[row, at]) for row, at in spots], sems.at[: rows + 1]
    )
    key_copies[0].wait()
    value_copies = start_copies(
        [(values_ref.at[row], values.at[row]) for row in range(rows)], sems.at[rows + 1 :]
    )
    scale = DH**-0.5
    heads, scores, new_scores, new_values = [], [], [], []
    for row in range(rows):
        at = q_cols + kv_cols
        line = sums_ref[row, 0:1, :]
        row_scale = lax.rsqrt((line[:, at : at + 1] + line[:, at + 1 : at + 2]) / D + EPS)
        q = (sums_ref[row, :, :q_cols] * row_scale).astype(BF16)
        fresh = (raw_ref[row : row + 1, :] * row_scale).astype(BF16).astype(F32)
        fresh_ref[row : row + 1, :] = fresh
        heads.append(jnp.concatenate([q[:, :DH], q[:, DH:]], axis=0))
        heads32 = heads[row].astype(F32)
        lines = [ref[row : row + 1, :] for ref in news] + [fresh]
        new_scores.append(
            [jnp.sum(heads32 * line[:, :DH], axis=1, keepdims=True) * scale for line in lines]
        )
        new_values.append([line[:, DH:] for line in lines])
    for copy in key_copies[1:]:
        copy.wait()
    for row in range(rows):
        old_s = lax.dot_general(
            heads[row], keys[row], (((1,), (1,)), ((), ())), preferred_element_type=F32
        )
        place = lax.broadcasted_iota(jnp.int32, old_s.shape, 1)
        scores.append(jnp.where(place < lengths_ref[row], old_s * scale, -jnp.inf))
    weights = []
    for row in range(rows):
        top = jnp.max(scores[row], axis=1, keepdims=True)
        for score in new_scores[row]:
            top = jnp.maximum(top, score)
        old_e = jnp.exp(scores[row] - top)
        new_e = [jnp.exp(score - top) for score in new_scores[row]]
        total = jnp.sum(old_e, axis=1, keepdims=True)
        for e in new_e:
            total = total + e
        share = 1.0 / total
        weights.append(((old_e * share).astype(BF16), [(e * share).astype(BF16) for e in new_e]))
    for copy in value_copies:
        copy.wait()
    for row in range(rows):
        old_w, new_w = weights[row]
        result = dot32(old_w, values[row])
        for w, v in zip(new_w, new_values[row]):
            result = result + w.astype(F32) * v
        out_ref[row] = jnp.concatenate([result[:count], result[count:]], axis=1).astype(BF16)


def attend(lengths, sums, raw, news, keys, values, kv_cols):
    rows, blocks, cols = sums.shape
    return call(
        functools.partial(attend_kernel, len(news) + 1, kv_cols),
        [
            jax.ShapeDtypeStruct((rows, blocks, cols - LANES), BF16),
            jax.ShapeDtypeStruct(raw.shape, F32),
        ],
        lengths,
        sums,
        raw,
        *news,
        keys,
        values,
        scalars=1,
        far=2,
        copies=2 * rows + 1,
        buffers=[pltpu.VMEM(keys.shape, BF16), pltpu.VMEM(values.shape, BF16)],
    )


def heads_kernel(blocks, heads_ref, wout_ref, down_ref, out_ref, held_ref, buffer, sems):
    width = out_ref.shape[1]
    block = width // blocks
    spots = [pl.ds(at, block) for at in range(0, width, block)]
    pairs = [(wout_ref.at[:, spot], buffer.at[:, spot]) for spot in spots]
    pairs += [(down_ref.at[:, spot], held_ref.at[:, spot]) for spot in spots]
    copies = start_copies(pairs, sems)
    for n, spot in enumerate(spots):
        copies[n].wait()
        out_ref[:, spot] = dot32(heads_ref[...], buffer[:, spot])
    for copy in copies[blocks:]:
        copy.wait()


def heads_output(heads, w_out, w_down, blocks=4):
    width = w_out.shape[1]
    return call(
        functools.partial(heads_kernel, blocks),
        [
            jax.ShapeDtypeStruct((heads.shape[0], width), F32),
            pltpu.VMEM(w_down.shape, w_down.dtype),
        ],
        heads,
        w_out,
        w_down,
        far=2,
        copies=2 * blocks,
        buffers=[pltpu.VMEM(w_out.shape, BF16)],
        cost=LATE,
    )


def output_kernel(gz, block, core_flip, place_ref, *refs):
    pieces = refs[:gz]
    part_ref, down_ref, out_ref, hidden = refs[gz:]
    size, half = pieces[0].shape
    z = place_ref[0]
    core = 1 - place_ref[1] if core_flip else place_ref[1]
    here = pl.ds(pl.multiple_of(core * half, half), half)
    for n in range(gz):
        at = pl.ds(pl.multiple_of(lax.rem(z + gz - n, gz) * size, size), size)
        hidden[at, :] = pieces[n][...]
    for at in range(0, out_ref.shape[1], block):
        out_ref[:, at : at + block] = (
            dot32(hidden[...], down_ref[here, at : at + block]) + part_ref[:, at : at + block]
        ).astype(out_ref.dtype)


def output_part(place, pieces, part, w_down, core_flip, dtype):
    return call(
        functools.partial(output_kernel, len(pieces), 512, core_flip),
        jax.ShapeDtypeStruct(part.shape, dtype),
        place,
        *pieces,
        part,
        w_down,
        scalars=1,
        buffers=[pltpu.VMEM((part.shape[0], w_down.shape[0] // 2), BF16)],
    )


def make_body(gx, gy):
    gz = gx // 2
    core_swap = [(n, n ^ 1) for n in range(gx)]

    def z_shift(n):
        return [(2 * z + c, 2 * ((z + n) % gz) + c) for z in range(gz) for c in range(2)]

    def exchange(parts, axis):
        return lax.all_to_all(parts, axis, split_axis=0, concat_axis=0, tiled=False)

    def body(
        residual,
        norm_gain,
        w_gate,
        w_up,
        w_query,
        w_keyval,
        w_down,
        w_out,
        cache_keys,
        cache_values,
        lengths,
    ):
        own_rows, width = residual.shape
        rows = own_rows * gy
        half = w_gate.shape[1] // 2
        q_cols = w_query.shape[1]
        kv_cols = w_keyval.shape[1]
        cache_rows = cache_keys.shape[0]
        me = lax.axis_index("gx")
        z, core = me // 2, lax.rem(me, 2)
        place = jnp.stack([z, core]).astype(jnp.int32)
        stream, place, mine_half, other_half = lax.optimization_barrier(
            (residual, place, place[1:], place[1:] ^ 1)
        )
        gain = norm_gain[None, :]
        news = []
        spread, held_query = call(
            spread_kernel,
            [
                jax.ShapeDtypeStruct((gy, own_rows, width), BF16),
                pltpu.VMEM(w_query.shape, w_query.dtype),
            ],
            stream,
            gain,
            w_query,
            far=3,
            copies=3,
            buffers=[pltpu.VMEM(stream.shape, F32), pltpu.VMEM(gain.shape, F32)],
            cost=LATE,
        )
        for step in range(STEPS):
            gathered = exchange(spread, "gy").reshape(rows, width)
            packed, squares = call(
                query_kernel,
                (
                    jax.ShapeDtypeStruct((rows, q_cols + LANES), BF16),
                    jax.ShapeDtypeStruct((rows, LANES), BF16),
                ),
                gathered,
                gain,
                w_keyval.T,
                held_query if step == 0 else w_query,
            )
            give = hidden_part(other_half, gathered, w_gate, w_up)
            other = [lax.ppermute(part, "gx", core_swap) for part in (*give, squares)]
            keep = hidden_part(mine_half, gathered, w_gate, w_up)
            packed = lax.optimization_barrier((packed, give, keep))[0]
            packed = exchange(
                packed.reshape(gx * gy, cache_rows, q_cols + LANES), ("gx", "gy")
            )
            pair = call(
                functools.partial(pair_kernel, gz),
                [jax.ShapeDtypeStruct((rows // gz, 2 * half + LANES), BF16)] * gz,
                place,
                *keep,
                squares,
                *other,
                scalars=1,
            )
            arrived = [pair[0]] + [lax.ppermute(pair[n], "gx", z_shift(n)) for n in range(1, gz)]

            packed = lax.optimization_barrier((packed, pair[0]))[0]
            mine = jnp.sum(
                packed.reshape(gx, gy, cache_rows, q_cols + LANES).astype(F32), axis=0
            ).transpose(1, 0, 2)
            at = q_cols + kv_cols
            raw = mine[:, :, q_cols:at].reshape(cache_rows, 2 * DH)
            attended, fresh = attend(
                lengths, mine, raw, news, cache_keys, cache_values, kv_cols
            )
            news.append(fresh)
            blocks = attended.transpose(1, 0, 2)
            blocks = jnp.broadcast_to(blocks[None], (gx, gy, cache_rows, q_cols))
            blocks = blocks.reshape(gx * gy, cache_rows, q_cols)
            heads_all = exchange(blocks, ("gx", "gy")).reshape(rows, q_cols)
            arrived = lax.optimization_barrier((arrived, blocks))[0]
            hidden = call(
                functools.partial(hidden_kernel, kv_cols),
                jax.ShapeDtypeStruct((rows // gz, half), BF16),
                *arrived,
            )
            pieces = [hidden] + [lax.ppermute(hidden, "gx", z_shift(n)) for n in range(1, gz)]
            own_other = lax.ppermute(hidden, "gx", core_swap)
            heads_all = lax.optimization_barrier((heads_all, own_other))[0]
            heads_part, held_down = heads_output(heads_all, w_out, w_down)
            late = lax.optimization_barrier((pieces[1:], heads_part))[0]
            others = [own_other] + [lax.ppermute(piece, "gx", core_swap) for piece in late]
            part = output_part(place, pieces, heads_part, held_down, False, F32)
            delta = output_part(place, others, part, held_down, True, BF16)
            delta = exchange(delta.reshape(gy, own_rows, width), "gy")
            stream_shape = jax.ShapeDtypeStruct(stream.shape, F32)
            spread_shape = jax.ShapeDtypeStruct((gy, own_rows, width), BF16)
            if step + 1 < STEPS:
                stream, spread = call(
                    add_kernel, (stream_shape, spread_shape), stream, delta, gain
                )
            else:
                stream = call(add_kernel, stream_shape, stream, delta, gain)
        return stream

    return body


def solution(mesh):
    in_specs = (
        P("gy", "gx"),
        P("gx"),
        P("gx", "gy"),
        P("gx", "gy"),
        P("gx", "gy"),
        P("gx", "gy"),
        P("gy", "gx"),
        P("gy", "gx"),
        P(("gx", "gy"), None, None),
        P(("gx", "gy"), None, None),
        P(("gx", "gy")),
    )
    return jax.shard_map(
        make_body(mesh.shape["gx"], mesh.shape["gy"]),
        mesh=mesh,
        in_specs=in_specs,
        out_specs=P("gy", "gx"),
        check_vma=False,
    )
```

```python
import functools

import jax
import jax.numpy as jnp
from jax import lax
from jax.experimental import pallas as pl
from jax.experimental.pallas import tpu as pltpu
from jax.sharding import PartitionSpec as P

D = 8192
HEADS = 32
DH = 256
STEPS = 2
EPS = 1e-06
LANES = 128
FIRST = 16
F32 = jnp.float32
BF16 = jnp.bfloat16
PARAMS = pltpu.CompilerParams(vmem_limit_bytes=16 * 1024 * 1024)
VMEM = pl.BlockSpec(memory_space=pltpu.VMEM)
SMEM = pl.BlockSpec(memory_space=pltpu.SMEM)
COST = pl.CostEstimate(flops=0, bytes_accessed=0, transcendentals=0)
LATE = pl.CostEstimate(flops=10**10, bytes_accessed=0, transcendentals=0)


def dot32(a, b):
    return jnp.dot(a, b, preferred_element_type=F32)


HBM = pl.BlockSpec(memory_space=pltpu.HBM)


def call(kernel, out_shape, *args, scalars=0, far=0, copies=0, buffers=(), cost=COST):
    near = len(args) - scalars - far
    far_args = [pltpu.with_memory_space_constraint(a, pltpu.HBM) for a in args[scalars + near :]]
    scratch = list(buffers)
    if copies:
        scratch.append(pltpu.SemaphoreType.DMA((copies,)))
    return pl.pallas_call(
        kernel,
        out_shape=out_shape,
        in_specs=[SMEM] * scalars + [VMEM] * near + [HBM] * far,
        scratch_shapes=scratch,
        compiler_params=PARAMS,
        cost_estimate=cost,
    )(*args[: scalars + near], *far_args)


def start_copies(pairs, sems):
    copies = [
        pltpu.make_async_copy(source, target, sems.at[n]) for n, (source, target) in enumerate(pairs)
    ]
    for copy in copies:
        copy.start()
    return copies


def spread_kernel(x_ref, gain_ref, out_ref, x, gain, sems):
    for copy in start_copies([(x_ref, x), (gain_ref, gain)], sems):
        copy.wait()
    scaled = (x[...] * gain[...]).astype(BF16)
    for n in range(out_ref.shape[0]):
        out_ref[n] = scaled


def add_kernel(x_ref, delta_ref, gain_ref, new_ref, out_ref=None):
    new = x_ref[...] + jnp.sum(delta_ref[...].astype(F32), axis=0)
    new_ref[...] = new
    if out_ref is not None:
        scaled = (new * gain_ref[...]).astype(BF16)
        for n in range(out_ref.shape[0]):
            out_ref[n] = scaled


def query_kernel(x_ref, gain_ref, wkv_ref, wq_ref, out_ref, squares_ref):
    x = x_ref[...]
    kv_cols, depth = wkv_ref.shape
    plain = x.astype(F32) * (1.0 / gain_ref[...])
    squares = jnp.sum(plain * plain, axis=1, keepdims=True)
    high = squares.astype(BF16).astype(F32)
    low = squares - high
    lane = lax.broadcasted_iota(jnp.int32, squares_ref.shape, 1)
    columns = jnp.where(lane == kv_cols, high, jnp.where(lane == kv_cols + 1, low, 0.0))
    squares_ref[...] = columns.astype(BF16)
    q_cols = wq_ref.shape[1]
    out_ref[:, :q_cols] = dot32(x, wq_ref[...]).astype(BF16)
    wkv = jnp.concatenate([wkv_ref[...], jnp.zeros((LANES - kv_cols, depth), BF16)], axis=0)
    keyval = lax.dot_general(x, wkv, (((1,), (1,)), ((), ())), preferred_element_type=F32)
    out_ref[:, q_cols:] = (keyval + columns).astype(BF16)


def hidden_part_kernel(half_ref, x_ref, wg_ref, wu_ref, *outs):
    half = wg_ref.shape[1] // 2
    block = outs[0].shape[1]
    start = half_ref[0] * half
    for n in range(len(outs) // 2):
        here = pl.ds(pl.multiple_of(start + n * block, block), block)
        outs[2 * n][...] = dot32(x_ref[...], wg_ref[:, here]).astype(BF16)
        outs[2 * n + 1][...] = dot32(x_ref[...], wu_ref[:, here]).astype(BF16)


def hidden_part_and_fetch_kernel(half_ref, x_ref, wg_ref, wu_ref, far_ref, *refs):
    outs, (held_ref, sems) = refs[:-2], refs[-2:]
    (copy,) = start_copies([(far_ref, held_ref)], sems)
    hidden_part_kernel(half_ref, x_ref, wg_ref, wu_ref, *outs)
    copy.wait()


def hidden_part(half_index, x, w_gate, w_up, fetch=None, blocks=2):
    part = jax.ShapeDtypeStruct((x.shape[0], w_gate.shape[1] // 2 // blocks), BF16)
    args = (half_index, x, w_gate, w_up)
    if fetch is None:
        return call(hidden_part_kernel, [part] * (2 * blocks), *args, scalars=1)
    return call(
        hidden_part_and_fetch_kernel,
        [part] * (2 * blocks) + [pltpu.VMEM(fetch.shape, fetch.dtype)],
        *args,
        fetch,
        scalars=1,
        far=1,
        copies=1,
    )


def pair_kernel(gz, z_ref, *refs):
    outs = refs[-gz:]
    count = (len(refs) - gz) // 2
    half = sum(ref.shape[1] for ref in refs[: count - 1]) // 2
    size = outs[0].shape[0]
    for n in range(gz):
        here = pl.ds(pl.multiple_of(lax.rem(z_ref[0] + n, gz) * size, size), size)
        for k in range(count):
            keep, other = refs[k], refs[count + k]
            block = keep.shape[1]
            at = 2 * half if k == count - 1 else k % 2 * half + k // 2 * block
            outs[n][:, at : at + block] = (
                keep[here, :].astype(F32) + other[here, :].astype(F32)
            ).astype(BF16)


def hidden_kernel(kv_cols, *refs):
    out_ref = refs[-1]
    half = out_ref.shape[1]
    total = refs[0][...].astype(F32)
    for ref in refs[1:-1]:
        total = total + ref[...].astype(F32)
    at = 2 * half + kv_cols
    scale = lax.rsqrt((total[:, at : at + 1] + total[:, at + 1 : at + 2]) / D + EPS)
    gate = total[:, :half] * scale
    up = total[:, half : 2 * half] * scale
    out_ref[...] = (gate / (1.0 + jnp.exp(-gate)) * up).astype(BF16)


def attend_kernel(steps, kv_cols, lengths_ref, sums_ref, raw_ref, *refs):
    news = refs[: steps - 1]
    keys_ref, values_ref, out_ref, fresh_ref, keys, values, sems = refs[steps - 1 :]
    rows, count = sums_ref.shape[:2]
    q_cols = sums_ref.shape[2] - LANES
    first = pl.ds(0, FIRST)
    rest = pl.ds(FIRST, keys.shape[1] - FIRST)
    spots = [(0, first), (0, rest)] + [(row, pl.ds(0, keys.shape[1])) for row in range(1, rows)]
    key_copies = start_copies(
        [(keys_ref.at[row, at], keys.at[row, at]) for row, at in spots], sems.at[: rows + 1]
    )
    key_copies[0].wait()
    value_copies = start_copies(
        [(values_ref.at[row], values.at[row]) for row in range(rows)], sems.at[rows + 1 :]
    )
    scale = DH**-0.5
    heads, scores, new_scores, new_values = [], [], [], []
    for row in range(rows):
        at = q_cols + kv_cols
        line = sums_ref[row, 0:1, :]
        row_scale = lax.rsqrt((line[:, at : at + 1] + line[:, at + 1 : at + 2]) / D + EPS)
        q = (sums_ref[row, :, :q_cols] * row_scale).astype(BF16)
        fresh = (raw_ref[row : row + 1, :] * row_scale).astype(BF16).astype(F32)
        fresh_ref[row : row + 1, :] = fresh
        heads.append(jnp.concatenate([q[:, :DH], q[:, DH:]], axis=0))
        heads32 = heads[row].astype(F32)
        lines = [ref[row : row + 1, :] for ref in news] + [fresh]
        new_scores.append(
            [jnp.sum(heads32 * line[:, :DH], axis=1, keepdims=True) * scale for line in lines]
        )
        new_values.append([line[:, DH:] for line in lines])
    for copy in key_copies[1:]:
        copy.wait()
    for row in range(rows):
        old_s = lax.dot_general(
            heads[row], keys[row], (((1,), (1,)), ((), ())), preferred_element_type=F32
        )
        place = lax.broadcasted_iota(jnp.int32, old_s.shape, 1)
        scores.append(jnp.where(place < lengths_ref[row], old_s * scale, -jnp.inf))
    weights = []
    for row in range(rows):
        top = jnp.max(scores[row], axis=1, keepdims=True)
        for score in new_scores[row]:
            top = jnp.maximum(top, score)
        old_e = jnp.exp(scores[row] - top)
        new_e = [jnp.exp(score - top) for score in new_scores[row]]
        total = jnp.sum(old_e, axis=1, keepdims=True)
        for e in new_e:
            total = total + e
        share = 1.0 / total
        weights.append(((old_e * share).astype(BF16), [(e * share).astype(BF16) for e in new_e]))
    for copy in value_copies:
        copy.wait()
    for row in range(rows):
        old_w, new_w = weights[row]
        result = dot32(old_w, values[row])
        for w, v in zip(new_w, new_values[row]):
            result = result + w.astype(F32) * v
        out_ref[row] = jnp.concatenate([result[:count], result[count:]], axis=1).astype(BF16)


def attend(lengths, sums, raw, news, keys, values, kv_cols):
    rows, blocks, cols = sums.shape
    return call(
        functools.partial(attend_kernel, len(news) + 1, kv_cols),
        [
            jax.ShapeDtypeStruct((rows, blocks, cols - LANES), BF16),
            jax.ShapeDtypeStruct(raw.shape, F32),
        ],
        lengths,
        sums,
        raw,
        *news,
        keys,
        values,
        scalars=1,
        far=2,
        copies=2 * rows + 1,
        buffers=[pltpu.VMEM(keys.shape, BF16), pltpu.VMEM(values.shape, BF16)],
    )


def heads_kernel(blocks, heads_ref, wout_ref, down_ref, out_ref, held_ref, buffer, sems):
    width = out_ref.shape[1]
    block = width // blocks
    spots = [pl.ds(at, block) for at in range(0, width, block)]
    pairs = [(wout_ref.at[:, spot], buffer.at[:, spot]) for spot in spots]
    pairs += [(down_ref.at[:, spot], held_ref.at[:, spot]) for spot in spots]
    copies = start_copies(pairs, sems)
    for n, spot in enumerate(spots):
        copies[n].wait()
        out_ref[:, spot] = dot32(heads_ref[...], buffer[:, spot])
    for copy in copies[blocks:]:
        copy.wait()


def heads_output(heads, w_out, w_down, blocks=4):
    width = w_out.shape[1]
    return call(
        functools.partial(heads_kernel, blocks),
        [
            jax.ShapeDtypeStruct((heads.shape[0], width), F32),
            pltpu.VMEM(w_down.shape, w_down.dtype),
        ],
        heads,
        w_out,
        w_down,
        far=2,
        copies=2 * blocks,
        buffers=[pltpu.VMEM(w_out.shape, BF16)],
        cost=LATE,
    )


def output_kernel(gz, block, core_flip, place_ref, *refs):
    pieces = refs[:gz]
    part_ref, down_ref, out_ref, hidden = refs[gz:]
    size, half = pieces[0].shape
    z = place_ref[0]
    core = 1 - place_ref[1] if core_flip else place_ref[1]
    here = pl.ds(pl.multiple_of(core * half, half), half)
    for n in range(gz):
        at = pl.ds(pl.multiple_of(lax.rem(z + gz - n, gz) * size, size), size)
        hidden[at, :] = pieces[n][...]
    for at in range(0, out_ref.shape[1], block):
        out_ref[:, at : at + block] = (
            dot32(hidden[...], down_ref[here, at : at + block]) + part_ref[:, at : at + block]
        ).astype(out_ref.dtype)


def output_part(place, pieces, part, w_down, core_flip, dtype):
    return call(
        functools.partial(output_kernel, len(pieces), 512, core_flip),
        jax.ShapeDtypeStruct(part.shape, dtype),
        place,
        *pieces,
        part,
        w_down,
        scalars=1,
        buffers=[pltpu.VMEM((part.shape[0], w_down.shape[0] // 2), BF16)],
    )


def make_body(gx, gy):
    gz = gx // 2
    core_swap = [(n, n ^ 1) for n in range(gx)]

    def z_shift(n):
        return [(2 * z + c, 2 * ((z + n) % gz) + c) for z in range(gz) for c in range(2)]

    def exchange(parts, axis):
        return lax.all_to_all(parts, axis, split_axis=0, concat_axis=0, tiled=False)

    def body(
        residual,
        norm_gain,
        w_gate,
        w_up,
        w_query,
        w_keyval,
        w_down,
        w_out,
        cache_keys,
        cache_values,
        lengths,
    ):
        own_rows, width = residual.shape
        rows = own_rows * gy
        half = w_gate.shape[1] // 2
        q_cols = w_query.shape[1]
        kv_cols = w_keyval.shape[1]
        cache_rows = cache_keys.shape[0]
        me = lax.axis_index("gx")
        z, core = me // 2, lax.rem(me, 2)
        place = jnp.stack([z, core]).astype(jnp.int32)
        stream, place, mine_half, other_half = lax.optimization_barrier(
            (residual, place, place[1:], place[1:] ^ 1)
        )
        gain = norm_gain[None, :]
        news = []
        spread = call(
            spread_kernel,
            jax.ShapeDtypeStruct((gy, own_rows, width), BF16),
            stream,
            gain,
            far=2,
            copies=2,
            buffers=[pltpu.VMEM(stream.shape, F32), pltpu.VMEM(gain.shape, F32)],
            cost=LATE,
        )
        for step in range(STEPS):
            gathered = exchange(spread, "gy").reshape(rows, width)
            near_query = w_query
            give = hidden_part(other_half, gathered, w_gate, w_up, w_query if step == 0 else None)
            if step == 0:
                *give, near_query = give
            packed, squares = call(
                query_kernel,
                (
                    jax.ShapeDtypeStruct((rows, q_cols + LANES), BF16),
                    jax.ShapeDtypeStruct((rows, LANES), BF16),
                ),
                gathered,
                gain,
                w_keyval.T,
                near_query,
            )
            other = [lax.ppermute(part, "gx", core_swap) for part in (*give, squares)]
            keep = hidden_part(mine_half, gathered, w_gate, w_up)
            packed = lax.optimization_barrier((packed, give, keep))[0]
            packed = exchange(
                packed.reshape(gx * gy, cache_rows, q_cols + LANES), ("gx", "gy")
            )
            pair = call(
                functools.partial(pair_kernel, gz),
                [jax.ShapeDtypeStruct((rows // gz, 2 * half + LANES), BF16)] * gz,
                place,
                *keep,
                squares,
                *other,
                scalars=1,
            )
            arrived = [pair[0]] + [lax.ppermute(pair[n], "gx", z_shift(n)) for n in range(1, gz)]

            packed = lax.optimization_barrier((packed, pair[0]))[0]
            mine = jnp.sum(
                packed.reshape(gx, gy, cache_rows, q_cols + LANES).astype(F32), axis=0
            ).transpose(1, 0, 2)
            at = q_cols + kv_cols
            raw = mine[:, :, q_cols:at].reshape(cache_rows, 2 * DH)
            attended, fresh = attend(
                lengths, mine, raw, news, cache_keys, cache_values, kv_cols
            )
            news.append(fresh)
            blocks = attended.transpose(1, 0, 2)
            blocks = jnp.broadcast_to(blocks[None], (gx, gy, cache_rows, q_cols))
            blocks = blocks.reshape(gx * gy, cache_rows, q_cols)
            heads_all = exchange(blocks, ("gx", "gy")).reshape(rows, q_cols)
            arrived = lax.optimization_barrier((arrived, blocks))[0]
            hidden = call(
                functools.partial(hidden_kernel, kv_cols),
                jax.ShapeDtypeStruct((rows // gz, half), BF16),
                *arrived,
            )
            pieces = [hidden] + [lax.ppermute(hidden, "gx", z_shift(n)) for n in range(1, gz)]
            own_other = lax.ppermute(hidden, "gx", core_swap)
            heads_all = lax.optimization_barrier((heads_all, own_other))[0]
            heads_part, held_down = heads_output(heads_all, w_out, w_down)
            late = [lax.optimization_barrier((piece, heads_part))[0] for piece in pieces[1:]]
            others = [own_other] + [lax.ppermute(piece, "gx", core_swap) for piece in late]
            part = output_part(place, pieces, heads_part, held_down, False, F32)
            delta = output_part(place, others, part, held_down, True, BF16)
            delta = exchange(delta.reshape(gy, own_rows, width), "gy")
            stream_shape = jax.ShapeDtypeStruct(stream.shape, F32)
            spread_shape = jax.ShapeDtypeStruct((gy, own_rows, width), BF16)
            if step + 1 < STEPS:
                stream, spread = call(
                    add_kernel, (stream_shape, spread_shape), stream, delta, gain
                )
            else:
                stream = call(add_kernel, stream_shape, stream, delta, gain)
        return stream

    return body


def solution(mesh):
    in_specs = (
        P("gy", "gx"),
        P("gx"),
        P("gx", "gy"),
        P("gx", "gy"),
        P("gx", "gy"),
        P("gx", "gy"),
        P("gy", "gx"),
        P("gy", "gx"),
        P(("gx", "gy"), None, None),
        P(("gx", "gy"), None, None),
        P(("gx", "gy")),
    )
    return jax.shard_map(
        make_body(mesh.shape["gx"], mesh.shape["gy"]),
        mesh=mesh,
        in_specs=in_specs,
        out_specs=P("gy", "gx"),
        check_vma=False,
    )
```

```python
import functools

import jax
import jax.numpy as jnp
from jax import lax
from jax.experimental import pallas as pl
from jax.experimental.pallas import tpu as pltpu
from jax.sharding import PartitionSpec as P

D = 8192
HEADS = 32
DH = 256
STEPS = 2
EPS = 1e-06
LANES = 128
FIRST = 16
F32 = jnp.float32
BF16 = jnp.bfloat16
PARAMS = pltpu.CompilerParams(vmem_limit_bytes=16 * 1024 * 1024)
VMEM = pl.BlockSpec(memory_space=pltpu.VMEM)
SMEM = pl.BlockSpec(memory_space=pltpu.SMEM)
COST = pl.CostEstimate(flops=0, bytes_accessed=0, transcendentals=0)
LATE = pl.CostEstimate(flops=10**10, bytes_accessed=0, transcendentals=0)


def dot32(a, b):
    return jnp.dot(a, b, preferred_element_type=F32)


HBM = pl.BlockSpec(memory_space=pltpu.HBM)


def call(kernel, out_shape, *args, scalars=0, far=0, copies=0, buffers=(), cost=COST):
    near = len(args) - scalars - far
    far_args = [pltpu.with_memory_space_constraint(a, pltpu.HBM) for a in args[scalars + near :]]
    scratch = list(buffers)
    if copies:
        scratch.append(pltpu.SemaphoreType.DMA((copies,)))
    return pl.pallas_call(
        kernel,
        out_shape=out_shape,
        in_specs=[SMEM] * scalars + [VMEM] * near + [HBM] * far,
        scratch_shapes=scratch,
        compiler_params=PARAMS,
        cost_estimate=cost,
    )(*args[: scalars + near], *far_args)


def start_copies(pairs, sems):
    copies = [
        pltpu.make_async_copy(source, target, sems.at[n]) for n, (source, target) in enumerate(pairs)
    ]
    for copy in copies:
        copy.start()
    return copies


def spread_kernel(x_ref, gain_ref, out_ref, x, gain, sems):
    for copy in start_copies([(x_ref, x), (gain_ref, gain)], sems):
        copy.wait()
    scaled = (x[...] * gain[...]).astype(BF16)
    for n in range(out_ref.shape[0]):
        out_ref[n] = scaled


def add_kernel(x_ref, delta_ref, gain_ref, new_ref, out_ref=None):
    new = x_ref[...] + jnp.sum(delta_ref[...].astype(F32), axis=0)
    new_ref[...] = new
    if out_ref is not None:
        scaled = (new * gain_ref[...]).astype(BF16)
        for n in range(out_ref.shape[0]):
            out_ref[n] = scaled


def query_kernel(x_ref, gain_ref, wkv_ref, wq_ref, out_ref, squares_ref):
    x = x_ref[...]
    kv_cols, depth = wkv_ref.shape
    plain = x.astype(F32) * (1.0 / gain_ref[...])
    squares = jnp.sum(plain * plain, axis=1, keepdims=True)
    high = squares.astype(BF16).astype(F32)
    low = squares - high
    lane = lax.broadcasted_iota(jnp.int32, squares_ref.shape, 1)
    columns = jnp.where(lane == kv_cols, high, jnp.where(lane == kv_cols + 1, low, 0.0))
    squares_ref[...] = columns.astype(BF16)
    q_cols = wq_ref.shape[1]
    out_ref[:, :q_cols] = dot32(x, wq_ref[...]).astype(BF16)
    wkv = jnp.concatenate([wkv_ref[...], jnp.zeros((LANES - kv_cols, depth), BF16)], axis=0)
    keyval = lax.dot_general(x, wkv, (((1,), (1,)), ((), ())), preferred_element_type=F32)
    out_ref[:, q_cols:] = (keyval + columns).astype(BF16)


def hidden_part_kernel(half_ref, x_ref, wg_ref, wu_ref, *outs):
    half = wg_ref.shape[1] // 2
    block = outs[0].shape[1]
    start = half_ref[0] * half
    for n in range(len(outs) // 2):
        here = pl.ds(pl.multiple_of(start + n * block, block), block)
        outs[2 * n][...] = dot32(x_ref[...], wg_ref[:, here]).astype(BF16)
        outs[2 * n + 1][...] = dot32(x_ref[...], wu_ref[:, here]).astype(BF16)


def hidden_part_and_fetch_kernel(half_ref, x_ref, wg_ref, wu_ref, far_ref, *refs):
    outs, (held_ref, sems) = refs[:-2], refs[-2:]
    (copy,) = start_copies([(far_ref, held_ref)], sems)
    hidden_part_kernel(half_ref, x_ref, wg_ref, wu_ref, *outs)
    copy.wait()


def hidden_part(half_index, x, w_gate, w_up, fetch=None, blocks=2):
    part = jax.ShapeDtypeStruct((x.shape[0], w_gate.shape[1] // 2 // blocks), BF16)
    args = (half_index, x, w_gate, w_up)
    if fetch is None:
        return call(hidden_part_kernel, [part] * (2 * blocks), *args, scalars=1)
    return call(
        hidden_part_and_fetch_kernel,
        [part] * (2 * blocks) + [pltpu.VMEM(fetch.shape, fetch.dtype)],
        *args,
        fetch,
        scalars=1,
        far=1,
        copies=1,
    )


def pair_kernel(gz, z_ref, *refs):
    outs = refs[-gz:]
    count = (len(refs) - gz) // 2
    half = sum(ref.shape[1] for ref in refs[: count - 1]) // 2
    size = outs[0].shape[0]
    for n in range(gz):
        here = pl.ds(pl.multiple_of(lax.rem(z_ref[0] + n, gz) * size, size), size)
        for k in range(count):
            keep, other = refs[k], refs[count + k]
            block = keep.shape[1]
            at = 2 * half if k == count - 1 else k % 2 * half + k // 2 * block
            outs[n][:, at : at + block] = (
                keep[here, :].astype(F32) + other[here, :].astype(F32)
            ).astype(BF16)


def hidden_kernel(kv_cols, *refs):
    out_ref = refs[-1]
    half = out_ref.shape[1]
    total = refs[0][...].astype(F32)
    for ref in refs[1:-1]:
        total = total + ref[...].astype(F32)
    at = 2 * half + kv_cols
    scale = lax.rsqrt((total[:, at : at + 1] + total[:, at + 1 : at + 2]) / D + EPS)
    gate = total[:, :half] * scale
    up = total[:, half : 2 * half] * scale
    out_ref[...] = (gate / (1.0 + jnp.exp(-gate)) * up).astype(BF16)


def attend_kernel(steps, kv_cols, lengths_ref, sums_ref, raw_ref, *refs):
    news = refs[: steps - 1]
    keys_ref, values_ref, out_ref, fresh_ref, keys, values, sems = refs[steps - 1 :]
    rows, count = sums_ref.shape[:2]
    q_cols = sums_ref.shape[2] - LANES
    first = pl.ds(0, FIRST)
    rest = pl.ds(FIRST, keys.shape[1] - FIRST)
    spots = [(0, first), (0, rest)] + [(row, pl.ds(0, keys.shape[1])) for row in range(1, rows)]
    key_copies = start_copies(
        [(keys_ref.at[row, at], keys.at[row, at]) for row, at in spots], sems.at[: rows + 1]
    )
    key_copies[0].wait()
    value_copies = start_copies(
        [(values_ref.at[row], values.at[row]) for row in range(rows)], sems.at[rows + 1 :]
    )
    scale = DH**-0.5
    heads, scores, new_scores, new_values = [], [], [], []
    for row in range(rows):
        at = q_cols + kv_cols
        line = sums_ref[row, 0:1, :]
        row_scale = lax.rsqrt((line[:, at : at + 1] + line[:, at + 1 : at + 2]) / D + EPS)
        q = (sums_ref[row, :, :q_cols] * row_scale).astype(BF16)
        fresh = (raw_ref[row : row + 1, :] * row_scale).astype(BF16).astype(F32)
        fresh_ref[row : row + 1, :] = fresh
        heads.append(jnp.concatenate([q[:, :DH], q[:, DH:]], axis=0))
        heads32 = heads[row].astype(F32)
        lines = [ref[row : row + 1, :] for ref in news] + [fresh]
        new_scores.append(
            [jnp.sum(heads32 * line[:, :DH], axis=1, keepdims=True) * scale for line in lines]
        )
        new_values.append([line[:, DH:] for line in lines])
    for row in range(rows):
        key_copies[row + 1].wait()
        old_s = lax.dot_general(
            heads[row], keys[row], (((1,), (1,)), ((), ())), preferred_element_type=F32
        )
        place = lax.broadcasted_iota(jnp.int32, old_s.shape, 1)
        scores.append(jnp.where(place < lengths_ref[row], old_s * scale, -jnp.inf))
    weights = []
    for row in range(rows):
        top = jnp.max(scores[row], axis=1, keepdims=True)
        for score in new_scores[row]:
            top = jnp.maximum(top, score)
        old_e = jnp.exp(scores[row] - top)
        new_e = [jnp.exp(score - top) for score in new_scores[row]]
        total = jnp.sum(old_e, axis=1, keepdims=True)
        for e in new_e:
            total = total + e
        share = 1.0 / total
        weights.append(((old_e * share).astype(BF16), [(e * share).astype(BF16) for e in new_e]))
    for row in range(rows):
        value_copies[row].wait()
        old_w, new_w = weights[row]
        result = dot32(old_w, values[row])
        for w, v in zip(new_w, new_values[row]):
            result = result + w.astype(F32) * v
        out_ref[row] = jnp.concatenate([result[:count], result[count:]], axis=1).astype(BF16)


def attend(lengths, sums, raw, news, keys, values, kv_cols):
    rows, blocks, cols = sums.shape
    return call(
        functools.partial(attend_kernel, len(news) + 1, kv_cols),
        [
            jax.ShapeDtypeStruct((rows, blocks, cols - LANES), BF16),
            jax.ShapeDtypeStruct(raw.shape, F32),
        ],
        lengths,
        sums,
        raw,
        *news,
        keys,
        values,
        scalars=1,
        far=2,
        copies=2 * rows + 1,
        buffers=[pltpu.VMEM(keys.shape, BF16), pltpu.VMEM(values.shape, BF16)],
    )


def heads_kernel(blocks, heads_ref, wout_ref, down_ref, out_ref, held_ref, buffer, sems):
    width = out_ref.shape[1]
    block = width // blocks
    spots = [pl.ds(at, block) for at in range(0, width, block)]
    pairs = [(wout_ref.at[:, spot], buffer.at[:, spot]) for spot in spots]
    pairs += [(down_ref.at[:, spot], held_ref.at[:, spot]) for spot in spots]
    copies = start_copies(pairs, sems)
    for n, spot in enumerate(spots):
        copies[n].wait()
        out_ref[:, spot] = dot32(heads_ref[...], buffer[:, spot])
    for copy in copies[blocks:]:
        copy.wait()


def heads_output(heads, w_out, w_down, blocks=4):
    width = w_out.shape[1]
    return call(
        functools.partial(heads_kernel, blocks),
        [
            jax.ShapeDtypeStruct((heads.shape[0], width), F32),
            pltpu.VMEM(w_down.shape, w_down.dtype),
        ],
        heads,
        w_out,
        w_down,
        far=2,
        copies=2 * blocks,
        buffers=[pltpu.VMEM(w_out.shape, BF16)],
        cost=LATE,
    )


def output_kernel(gz, block, core_flip, place_ref, *refs):
    pieces = refs[:gz]
    part_ref, down_ref, out_ref, hidden = refs[gz:]
    size, half = pieces[0].shape
    z = place_ref[0]
    core = 1 - place_ref[1] if core_flip else place_ref[1]
    here = pl.ds(pl.multiple_of(core * half, half), half)
    for n in range(gz):
        at = pl.ds(pl.multiple_of(lax.rem(z + gz - n, gz) * size, size), size)
        hidden[at, :] = pieces[n][...]
    for at in range(0, out_ref.shape[1], block):
        out_ref[:, at : at + block] = (
            dot32(hidden[...], down_ref[here, at : at + block]) + part_ref[:, at : at + block]
        ).astype(out_ref.dtype)


def output_part(place, pieces, part, w_down, core_flip, dtype):
    return call(
        functools.partial(output_kernel, len(pieces), 512, core_flip),
        jax.ShapeDtypeStruct(part.shape, dtype),
        place,
        *pieces,
        part,
        w_down,
        scalars=1,
        buffers=[pltpu.VMEM((part.shape[0], w_down.shape[0] // 2), BF16)],
    )


def make_body(gx, gy):
    gz = gx // 2
    core_swap = [(n, n ^ 1) for n in range(gx)]

    def z_shift(n):
        return [(2 * z + c, 2 * ((z + n) % gz) + c) for z in range(gz) for c in range(2)]

    def exchange(parts, axis):
        return lax.all_to_all(parts, axis, split_axis=0, concat_axis=0, tiled=False)

    def body(
        residual,
        norm_gain,
        w_gate,
        w_up,
        w_query,
        w_keyval,
        w_down,
        w_out,
        cache_keys,
        cache_values,
        lengths,
    ):
        own_rows, width = residual.shape
        rows = own_rows * gy
        half = w_gate.shape[1] // 2
        q_cols = w_query.shape[1]
        kv_cols = w_keyval.shape[1]
        cache_rows = cache_keys.shape[0]
        me = lax.axis_index("gx")
        z, core = me // 2, lax.rem(me, 2)
        place = jnp.stack([z, core]).astype(jnp.int32)
        stream, place, mine_half, other_half = lax.optimization_barrier(
            (residual, place, place[1:], place[1:] ^ 1)
        )
        gain = norm_gain[None, :]
        news = []
        spread = call(
            spread_kernel,
            jax.ShapeDtypeStruct((gy, own_rows, width), BF16),
            stream,
            gain,
            far=2,
            copies=2,
            buffers=[pltpu.VMEM(stream.shape, F32), pltpu.VMEM(gain.shape, F32)],
            cost=LATE,
        )
        for step in range(STEPS):
            gathered = exchange(spread, "gy").reshape(rows, width)
            near_query = w_query
            give = hidden_part(other_half, gathered, w_gate, w_up, w_query if step == 0 else None)
            if step == 0:
                *give, near_query = give
            packed, squares = call(
                query_kernel,
                (
                    jax.ShapeDtypeStruct((rows, q_cols + LANES), BF16),
                    jax.ShapeDtypeStruct((rows, LANES), BF16),
                ),
                gathered,
                gain,
                w_keyval.T,
                near_query,
            )
            other = [lax.ppermute(part, "gx", core_swap) for part in (*give, squares)]
            keep = hidden_part(mine_half, gathered, w_gate, w_up)
            packed = lax.optimization_barrier((packed, give, keep))[0]
            packed = exchange(
                packed.reshape(gx * gy, cache_rows, q_cols + LANES), ("gx", "gy")
            )
            pair = call(
                functools.partial(pair_kernel, gz),
                [jax.ShapeDtypeStruct((rows // gz, 2 * half + LANES), BF16)] * gz,
                place,
                *keep,
                squares,
                *other,
                scalars=1,
            )
            arrived = [pair[0]] + [lax.ppermute(pair[n], "gx", z_shift(n)) for n in range(1, gz)]

            packed = lax.optimization_barrier((packed, pair[0]))[0]
            mine = jnp.sum(
                packed.reshape(gx, gy, cache_rows, q_cols + LANES).astype(F32), axis=0
            ).transpose(1, 0, 2)
            at = q_cols + kv_cols
            raw = mine[:, :, q_cols:at].reshape(cache_rows, 2 * DH)
            attended, fresh = attend(
                lengths, mine, raw, news, cache_keys, cache_values, kv_cols
            )
            news.append(fresh)
            blocks = attended.transpose(1, 0, 2)
            blocks = jnp.broadcast_to(blocks[None], (gx, gy, cache_rows, q_cols))
            blocks = blocks.reshape(gx * gy, cache_rows, q_cols)
            heads_all = exchange(blocks, ("gx", "gy")).reshape(rows, q_cols)
            arrived = lax.optimization_barrier((arrived, blocks))[0]
            hidden = call(
                functools.partial(hidden_kernel, kv_cols),
                jax.ShapeDtypeStruct((rows // gz, half), BF16),
                *arrived,
            )
            pieces = [hidden] + [lax.ppermute(hidden, "gx", z_shift(n)) for n in range(1, gz)]
            own_other = lax.ppermute(hidden, "gx", core_swap)
            heads_all = lax.optimization_barrier((heads_all, own_other))[0]
            heads_part, held_down = heads_output(heads_all, w_out, w_down)
            late = [lax.optimization_barrier((piece, heads_part))[0] for piece in pieces[1:]]
            others = [own_other] + [lax.ppermute(piece, "gx", core_swap) for piece in late]
            part = output_part(place, pieces, heads_part, held_down, False, F32)
            delta = output_part(place, others, part, held_down, True, BF16)
            delta = exchange(delta.reshape(gy, own_rows, width), "gy")
            stream_shape = jax.ShapeDtypeStruct(stream.shape, F32)
            spread_shape = jax.ShapeDtypeStruct((gy, own_rows, width), BF16)
            if step + 1 < STEPS:
                stream, spread = call(
                    add_kernel, (stream_shape, spread_shape), stream, delta, gain
                )
            else:
                stream = call(add_kernel, stream_shape, stream, delta, gain)
        return stream

    return body


def solution(mesh):
    in_specs = (
        P("gy", "gx"),
        P("gx"),
        P("gx", "gy"),
        P("gx", "gy"),
        P("gx", "gy"),
        P("gx", "gy"),
        P("gy", "gx"),
        P("gy", "gx"),
        P(("gx", "gy"), None, None),
        P(("gx", "gy"), None, None),
        P(("gx", "gy")),
    )
    return jax.shard_map(
        make_body(mesh.shape["gx"], mesh.shape["gy"]),
        mesh=mesh,
        in_specs=in_specs,
        out_specs=P("gy", "gx"),
        check_vma=False,
    )
```
